256 devices in a mesh: section: 16 (over x_lo, y, core), dp: 16 (over x_hi, z).
Axes of the slice: x: 4 (x_hi: 2, x_lo: 2; x = x_hi * 2 + x_lo), y: 4, z: 8, core: 2. Of those that a mesh axis runs over, the one named last changes fastest.
Arguments:
- inputs: bfloat16 [2, 8, 128, 12288], P(None, None, 'dp'), may hold values from -6 to 6
- down_proj: bfloat16 [16, 24, 12288], P('section'), may hold values from -0.0546875 to 0.0546875
- up_proj: bfloat16 [16, 24, 12288], P('section'), may hold values from -1.25 to 1.25
Outputs:
- grad_down_proj: float32 [16, 24, 12288], P('section', None, 'dp')
- grad_up_proj: float32 [16, 24, 12288], P('section', None, 'dp')
The draws below stay inside these ranges and needn't reach their ends.
All inputs are finite; a program needn't handle non-finite values.
Results may differ from the reference program's by a relative error of at most 0.0075.
Values may be sent and summed in bfloat16 or wider, within the bound.
No kernel may reach another device: no remote copies, remote signals or barrier semaphores. Data moves between devices by JAX's collectives and lax.ppermute only.
A program may use at most 64 MiB of HBM per device.

```python
import jax
import jax.numpy as jnp
from jax import lax

D = 12288
RANK = 24
MICRO = 8
ROWS = 8
TOKENS = 128
BLOCKS = 16
N_SECTION = 16
N_DP = 16


def levels(rng, extent, cuts, smallest, largest):
    def one(dim, parts):
        heights = jax.random.uniform(jax.random.fold_in(jax.random.fold_in(rng, 6), dim), (parts,), jnp.float32, smallest / len(cuts), largest / len(cuts))
        return jnp.repeat(jnp.exp(heights), extent[dim] // parts).reshape((-1,) + (1,) * (len(extent) - dim - 1))

    gain = one(*cuts[0])
    for cut in cuts[1:]:
        gain = gain * one(*cut)
    return gain


def normal_values(stream_key, dims, spread, most, shards=(), dtype=jnp.bfloat16):
    gain = levels(stream_key, dims, shards, -0.22, 0.18) if shards else 1.0
    result = jax.random.normal(stream_key, dims, jnp.float32) * spread * gain
    return jnp.minimum(jnp.maximum(result, -most), most).astype(dtype)


def setup_inputs(seed: int = 0) -> dict:
    key_list = jax.random.split(jax.random.key(seed), 4)
    inputs = normal_values(key_list[0], (2, MICRO, TOKENS, D), 1.0, 6.0, ((2, 16),))
    down_proj = normal_values(key_list[1], (BLOCKS, RANK, D), D ** -0.5, 0.0546875, ((0, 16),))
    up_proj = normal_values(key_list[2], (BLOCKS, RANK, D), RANK ** -0.5, 1.25, ((0, 16),))
    return {"inputs": inputs, "down_proj": down_proj, "up_proj": up_proj}


EPS = 1e-05

def contract_features(first_operand, second_operand):
    return lax.dot_general(first_operand, second_operand, (((1,), (1,)), ((), ())), preferred_element_type=jnp.float32)

def layer_forward(hidden, proj_down, proj_up):
    hidden_f = hidden.astype(jnp.float32)
    inv_rms = lax.rsqrt(lax.optimization_barrier(jnp.mean(hidden_f * hidden_f, axis=-1, keepdims=True)) + EPS)
    normed = (hidden_f * inv_rms).astype(jnp.bfloat16)
    pre_act = contract_features(normed, proj_down)
    gated_act = jax.nn.silu(pre_act).astype(jnp.bfloat16)
    return (hidden_f + jnp.dot(gated_act, proj_up, preferred_element_type=jnp.float32)).astype(jnp.bfloat16)

def layer_backward(hidden, gradient, proj_down, proj_up):
    hidden_f = hidden.astype(jnp.float32)
    inv_rms = lax.rsqrt(lax.optimization_barrier(jnp.mean(hidden_f * hidden_f, axis=-1, keepdims=True)) + EPS)
    normed = (hidden_f * inv_rms).astype(jnp.bfloat16)
    pre_act = contract_features(normed, proj_down)
    gated_act = jax.nn.silu(pre_act).astype(jnp.bfloat16)
    grad_gated = contract_features(gradient, proj_up)
    sigmoid_val = jax.nn.sigmoid(pre_act)
    grad_pre = (grad_gated * sigmoid_val * (1.0 + pre_act * (1.0 - sigmoid_val))).astype(jnp.bfloat16)
    grad_normed = jnp.dot(grad_pre, proj_down, preferred_element_type=jnp.float32)
    feature_count = hidden_f.shape[-1]
    inner_sum = lax.optimization_barrier(jnp.sum(grad_normed * hidden_f, axis=-1, keepdims=True))
    grad_hidden = inv_rms * grad_normed - hidden_f * (inv_rms * inv_rms * inv_rms) * inner_sum / feature_count
    grad_in = (gradient.astype(jnp.float32) + grad_hidden).astype(jnp.bfloat16)
    return (grad_in, grad_pre, normed, gated_act)

def group_sums(first_operand, second_operand):
    first_rows = first_operand.reshape(2, MICRO, N_DP, ROWS, -1).astype(jnp.float32)
    second_rows = second_operand.reshape(2, MICRO, N_DP, ROWS, -1).astype(jnp.float32)
    partial_value = jnp.einsum('pmkrq,pmkrd->pkqd', first_rows, second_rows)
    return lax.optimization_barrier(jnp.sum(partial_value, axis=(0, 1)))

def reference(inputs, down_proj, up_proj):
    flat_rows = inputs.reshape(-1, inputs.shape[-1])
    saved_rows = []
    hidden = flat_rows
    for layer in range(N_SECTION):
        saved_rows.append(hidden)
        hidden = layer_forward(hidden, down_proj[layer], up_proj[layer])
    gradient = ((hidden.astype(jnp.float32) - flat_rows.astype(jnp.float32)) / (MICRO * TOKENS)).astype(jnp.bfloat16)
    grads_down = [None] * N_SECTION
    grads_up = [None] * N_SECTION
    for layer in reversed(range(N_SECTION)):
        grad_in, grad_pre, normed, gated_act = layer_backward(saved_rows[layer], gradient, down_proj[layer], up_proj[layer])
        grads_down[layer] = group_sums(grad_pre, normed)
        grads_up[layer] = group_sums(gated_act, gradient)
        gradient = grad_in
    return (jnp.stack(grads_down), jnp.stack(grads_up))
```

```python
import jax
import jax.numpy as jnp
from jax import lax
from jax.experimental import pallas as pl
from jax.experimental.pallas import tpu as pltpu
from jax.sharding import PartitionSpec as P

EPS = 1e-05
LANES = 128
F32 = jnp.float32
BF16 = jnp.bfloat16


def split(value):
    high = value.astype(BF16)
    return high, (value - high.astype(F32)).astype(BF16)


def dot_nn(left, right):
    return lax.dot_general(left, right, (((1,), (0,)), ((), ())), preferred_element_type=F32)


def dot_nt(left, right):
    return lax.dot_general(left, right, (((1,), (1,)), ((), ())), preferred_element_type=F32)


def params():
    return pltpu.CompilerParams(vmem_limit_bytes=48 * 1024 * 1024)


def project_kernel(x_ref, down_ref, up_ref, both_ref, square_ref, acc_ref, sum_ref):
    step = pl.program_id(0)

    @pl.when(step == 0)
    def _():
        acc_ref[...] = jnp.zeros_like(acc_ref)
        sum_ref[...] = jnp.zeros_like(sum_ref)

    rows = x_ref[...]
    rank = down_ref.shape[0]
    acc_ref[0:rank] += dot_nt(down_ref[...], rows)
    acc_ref[rank : 2 * rank] += dot_nt(up_ref[...], rows)
    wide = rows.astype(F32)
    total = sum_ref[...]
    for tile in range(wide.shape[1] // LANES):
        part = wide[:, tile * LANES : (tile + 1) * LANES]
        total += part * part
    sum_ref[...] = total

    @pl.when(step == pl.num_programs(0) - 1)
    def _():
        high, low = split(acc_ref[...])
        both_ref[...] = jnp.concatenate([high, low], axis=1)
        square_ref[...] = jnp.sum(sum_ref[...].T, axis=0, keepdims=True)


def project(rows, down, up):
    count, features = rows.shape
    rank = down.shape[0]
    width = features // 8
    return pl.pallas_call(
        project_kernel,
        grid=(8,),
        in_specs=[
            pl.BlockSpec((count, width), lambda c: (0, c)),
            pl.BlockSpec((rank, width), lambda c: (0, c)),
            pl.BlockSpec((rank, width), lambda c: (0, c)),
        ],
        out_specs=[
            pl.BlockSpec((2 * rank, 2 * LANES), lambda c: (0, 0)),
            pl.BlockSpec((1, LANES), lambda c: (0, 0)),
        ],
        out_shape=[
            jax.ShapeDtypeStruct((2 * rank, 2 * LANES), BF16),
            jax.ShapeDtypeStruct((1, LANES), F32),
        ],
        scratch_shapes=[pltpu.VMEM((2 * rank, LANES), F32), pltpu.VMEM((LANES, LANES), F32)],
        compiler_params=params(),
    )(rows, down, up)


def pair_kernel(own_ref, other_ref, out_ref, pad_ref):
    rank = own_ref.shape[0]
    pad_ref[...] = jnp.zeros_like(pad_ref)
    pad_ref[:, 0:rank] = dot_nt(own_ref[...], other_ref[...])
    packed = pad_ref[0:8]
    for group in range(1, rank // 8):
        packed += pltpu.roll(pad_ref[8 * group : 8 * group + 8], rank * group, 1)
    for copy in range(out_ref.shape[0]):
        out_ref[copy] = packed


def pair_products(own, other, copies):
    rank = own.shape[0]
    return pl.pallas_call(
        pair_kernel,
        out_shape=jax.ShapeDtypeStruct((copies, 8, LANES), F32),
        scratch_shapes=[pltpu.VMEM((rank, LANES), F32)],
        compiler_params=params(),
    )(own, other)


def order_kernel(rank, blocks, in_ref, out_ref):
    position = lax.axis_index("section")
    lane = lax.broadcasted_iota(jnp.int32, (8, LANES), 1)
    tiles = rank * blocks // LANES
    pieces = [in_ref[position ^ t] for t in range(blocks)]
    for group in range(rank // 8):
        turned = [pltpu.roll(pieces[t], (rank * (t - group)) % LANES, 1) for t in range(blocks)]
        for tile in range(tiles):
            place = (lane + tile * LANES) // rank
            value = jnp.zeros((8, LANES), F32)
            for t in range(blocks):
                if rank * t < (tile + 1) * LANES and rank * (t + 1) > tile * LANES:
                    value = jnp.where(place == t, turned[t], value)
            for copy in range(out_ref.shape[0]):
                out_ref[copy, tile * rank + 8 * group : tile * rank + 8 * group + 8] = value


def order_blocks(gathered, rank, copies):
    blocks = gathered.shape[0]

    def kernel(in_ref, out_ref):
        order_kernel(rank, blocks, in_ref, out_ref)

    rows = rank * blocks // LANES * rank
    return pl.pallas_call(
        kernel,
        out_shape=jax.ShapeDtypeStruct((copies, rows, LANES), F32),
        compiler_params=params(),
    )(gathered)


def chain_kernel(rank, blocks, features, normalizer, grid_ref, proj_ref, square_ref, out_ref, *rest):
    plain_ref, turned_ref, act_ref, scaled_ref, grad_ref, skip_ref = rest
    size = rank * blocks
    tiles = size // LANES
    whole = jnp.concatenate(
        [
            jnp.concatenate(
                [grid_ref[b, tile * rank : (tile + 1) * rank] for tile in range(tiles)], axis=1
            )
            for b in range(blocks)
        ],
        axis=0,
    )
    for ref, value in ((plain_ref, whole), (turned_ref, whole.T)):
        high, low = split(value)
        for tile in range(tiles):
            ref[:, 2 * tile * LANES : (2 * tile + 1) * LANES] = high[:, tile * LANES : (tile + 1) * LANES]
            ref[:, (2 * tile + 1) * LANES : (2 * tile + 2) * LANES] = low[
                :, tile * LANES : (tile + 1) * LANES
            ]

    def span(b):
        first = rank * b // LANES
        last = (rank * b + rank - 1) // LANES
        return first, last

    def columns(ref, b, start, stop):
        first, last = span(b)
        return ref[start:stop, 2 * first * LANES : 2 * (last + 1) * LANES]

    def placed(b, value):
        first, last = span(b)
        before = rank * b - first * LANES
        after = (last + 1) * LANES - rank * (b + 1)
        parts = []
        if before:
            parts.append(jnp.zeros((before, LANES), F32))
        parts.append(value)
        if after:
            parts.append(jnp.zeros((after, LANES), F32))
        wide = jnp.concatenate(parts, axis=0).astype(BF16)
        doubled = []
        for tile in range(last - first + 1):
            doubled += [wide[tile * LANES : (tile + 1) * LANES]] * 2
        return jnp.concatenate(doubled, axis=0)

    narrow, hidden = [], []
    for b in range(blocks):
        pair = proj_ref[b].astype(F32)
        joined = pair[:, 0:LANES] + pair[:, LANES : 2 * LANES]
        narrow.append(joined[0:rank])
        hidden.append(joined[rank : 2 * rank])
    initial = list(hidden)
    square = square_ref[...]
    inverses, acts, pres, slopes, ends = [], [], [], [], []
    for b in range(blocks):
        inverse = lax.rsqrt(square / features + EPS)
        pre = narrow[b] * inverse
        sigmoid = 1.0 / (1.0 + jnp.exp(-pre))
        act = (pre * sigmoid).astype(BF16).astype(F32)
        act_ref[rank * b : rank * (b + 1)] = act
        inverses.append(inverse)
        acts.append(act)
        pres.append(pre)
        slopes.append(sigmoid * (1.0 + pre * (1.0 - sigmoid)))
        right = placed(b, act)
        if b + 1 < blocks:
            start = rank * (b + 1) // 16 * 16
            update = dot_nn(columns(turned_ref, b, start, size), right)
            for k in range(b + 1, blocks):
                narrow[k] = narrow[k] + update[rank * k - start : rank * (k + 1) - start]
        start = rank * b // 16 * 16
        update = dot_nn(columns(plain_ref, b, start, size), right)
        own = update[rank * b - start : rank * (b + 1) - start]
        for k in range(b + 1, blocks):
            hidden[k] = hidden[k] + update[rank * k - start : rank * (k + 1) - start]
        square = square + jnp.sum(act * (2.0 * hidden[b] + own), axis=0, keepdims=True)
        ends.append(hidden[b] + own)

    back = [jnp.zeros((rank, LANES), F32) for _ in range(blocks)]
    decay = jnp.zeros((1, LANES), F32)
    for k in reversed(range(blocks)):
        weight = 1.0 / normalizer - decay
        scaled = acts[k] * weight
        scaled_ref[rank * k : rank * (k + 1)] = scaled
        skip_ref[rank * k : rank * (k + 1)] = -decay * acts[k]
        incoming = ends[k] * weight - initial[k] / normalizer + back[k]
        grad = (incoming * slopes[k] * inverses[k]).astype(BF16).astype(F32)
        grad_ref[rank * k : rank * (k + 1)] = grad
        decay = decay + inverses[k] / features * jnp.sum(grad * pres[k], axis=0, keepdims=True)
        if k:
            stop = -(-rank * k // 16) * 16
            coarse = scaled.astype(BF16).astype(F32)
            fine = scaled - coarse
            update = (
                dot_nn(columns(turned_ref, k, 0, stop), placed(k, coarse))
                + dot_nn(columns(turned_ref, k, 0, stop), placed(k, fine))
                + dot_nn(columns(plain_ref, k, 0, stop), placed(k, grad))
            )
            for b in range(k):
                back[b] = back[b] + update[rank * b : rank * (b + 1)]

    position = lax.axis_index("section")
    mine = pl.ds(pl.multiple_of(position * rank, 8), rank)
    own_act = act_ref[mine].astype(BF16)
    own_high, own_low = split(scaled_ref[mine])
    own_grad = grad_ref[mine].astype(BF16)
    all_act = act_ref[...].astype(BF16)
    all_high, all_low = split(scaled_ref[...])
    all_grad = grad_ref[...].astype(BF16)
    place = lax.broadcasted_iota(jnp.int32, (rank, size), 1) // rank
    later = dot_nt(own_act, all_high) + dot_nt(own_act, all_low)
    earlier = dot_nt(own_high, all_act) + dot_nt(own_low, all_act)
    both_up = jnp.where(place >= position, later, earlier)
    crossed = jnp.where(
        place < position,
        dot_nt(own_grad, all_act),
        jnp.where(place > position, dot_nt(own_act, all_grad), 0.0),
    )
    pieces = [grad_ref[mine], skip_ref[mine]]
    for value in (both_up, crossed):
        pieces += [value[:, tile * LANES : (tile + 1) * LANES] for tile in range(tiles)]
    payload = jnp.concatenate(pieces, axis=0).astype(BF16)
    for copy in range(out_ref.shape[0]):
        out_ref[copy] = payload


def run_chain(grid, gathered, square, rank, features, normalizer, copies):
    blocks = grid.shape[0]
    size = rank * blocks
    rows = 2 * rank + 2 * (size // LANES) * rank

    def kernel(*refs):
        chain_kernel(rank, blocks, features, normalizer, *refs)

    last = gathered.shape[2] // (2 * LANES) - 1
    narrow = pltpu.VMEM((size, LANES), F32)
    return pl.pallas_call(
        kernel,
        grid=(1,),
        in_specs=[
            pl.BlockSpec(grid.shape, lambda i: (0, 0, 0)),
            pl.BlockSpec((blocks, 2 * rank, 2 * LANES), lambda i: (0, 0, last)),
            pl.BlockSpec((1, LANES), lambda i: (0, 0)),
        ],
        out_specs=pl.BlockSpec((copies, rows, LANES), lambda i: (0, 0, 0)),
        out_shape=jax.ShapeDtypeStruct((copies, rows, LANES), BF16),
        scratch_shapes=[
            pltpu.VMEM((size, 2 * size), BF16),
            pltpu.VMEM((size, 2 * size), BF16),
            narrow,
            narrow,
            narrow,
            narrow,
        ],
        compiler_params=params(),
    )(grid, gathered, square)


def finish_kernel(rank, blocks, parts_ref, rows_ref, weights_ref, down_ref, up_ref):
    size = rank * blocks
    tiles = size // LANES
    members = parts_ref.shape[0]
    position = lax.axis_index("section")
    total = None
    left = []
    for member in range(members):
        piece = parts_ref[member]
        left.append(piece[0 : 2 * rank])
        sums = piece.astype(F32)[2 * rank :]
        total = sums if total is None else total + sums

    def unfold(first):
        return jnp.concatenate(
            [total[(first + tile) * rank : (first + tile + 1) * rank] for tile in range(tiles)], axis=1
        )

    both_up, crossed = unfold(0), unfold(tiles)
    place = lax.broadcasted_iota(jnp.int32, (rank, size), 1) // rank
    below = jnp.where(place < position, crossed, 0.0)
    above = jnp.where(place > position, crossed, 0.0)
    weights = [weights_ref[b].astype(F32) for b in range(blocks)]
    all_down = jnp.concatenate([w[0:rank] for w in weights], axis=0).astype(BF16)
    all_up = jnp.concatenate([w[rank : 2 * rank] for w in weights], axis=0).astype(BF16)
    result = jnp.zeros((2 * rank, rows_ref.shape[2]), F32)
    for member in range(members):
        result += dot_nn(left[member], rows_ref[member])
    high, low = split(jnp.concatenate([below, both_up], axis=0))
    result += dot_nn(high, all_up) + dot_nn(low, all_up)
    high, low = split(above)
    cross = dot_nn(high, all_down) + dot_nn(low, all_down)
    down_ref[0] = result[0:rank]
    up_ref[0] = result[rank : 2 * rank] + cross


def finish(parts, rows, gathered, rank):
    blocks = gathered.shape[0]
    width = rows.shape[2]

    def kernel(*refs):
        finish_kernel(rank, blocks, *refs)

    shape = jax.ShapeDtypeStruct((1, rank, width), F32)
    out = pl.BlockSpec((1, rank, width), lambda i: (0, 0, 0))
    return pl.pallas_call(
        kernel,
        grid=(1,),
        in_specs=[
            pl.BlockSpec(parts.shape, lambda i: (0, 0, 0)),
            pl.BlockSpec(rows.shape, lambda i: (0, 0, 0)),
            pl.BlockSpec((blocks, 2 * rank, width), lambda i: (0, 0, 0)),
        ],
        out_specs=[out, out],
        out_shape=[shape, shape],
        compiler_params=params(),
    )(parts, rows, gathered)


def shards(inputs, down_proj, up_proj):
    sections = lax.axis_size("section")
    members = lax.axis_size("dp")
    position = lax.axis_index("section")
    member = lax.axis_index("dp")
    own_down, own_up = down_proj[0], up_proj[0]
    rank, features = own_down.shape
    width = features // members
    pipes, micro, count = inputs.shape[:3]
    normalizer = float(micro * count * members)
    all_rows = inputs.reshape(pipes * micro * count, features)

    route = [
        ((s ^ d) * members + d, s * members + d) for s in range(sections) for d in range(members)
    ]
    outgoing = jnp.where((position ^ member) >= position, own_up, own_down)
    other = lax.ppermute(outgoing, ("section", "dp"), route)

    share = lax.dynamic_index_in_dim(
        inputs.reshape(sections, count, features), position, 0, keepdims=False
    )
    share = share.reshape(count, members, width).transpose(1, 0, 2)
    share = lax.all_to_all(share, "dp", 0, 0)
    slices = lax.all_gather(share, "section")
    slices = slices.transpose(1, 0, 2, 3).reshape(members, sections * count, width)

    both, square = project(all_rows, own_down, own_up)
    own_slice = jnp.concatenate(
        [lax.dynamic_slice_in_dim(w, member * width, width, 1) for w in (own_down, own_up)], axis=0
    )
    gathered = lax.all_gather(jnp.concatenate([own_slice, both], axis=1), "section")

    products = lax.all_to_all(pair_products(own_up, other, members), "dp", 0, 0)
    grid = lax.all_to_all(order_blocks(products, rank, sections), "section", 0, 0)
    parts = run_chain(grid, gathered, square, rank, features, normalizer, members)
    parts = lax.all_to_all(parts, "dp", 0, 0)
    return finish(parts, slices, gathered, rank)


def solution(mesh):
    placed = (P(None, None, "dp", None), P("section", None, None), P("section", None, None))
    return jax.shard_map(
        shards,
        mesh=mesh,
        in_specs=placed,
        out_specs=(P("section", None, "dp"), P("section", None, "dp")),
        check_vma=False,
    )
```

```python
import jax
import jax.numpy as jnp
from jax import lax
from jax.experimental import pallas as pl
from jax.experimental.pallas import tpu as pltpu
from jax.sharding import PartitionSpec as P

EPS = 1e-05
LANES = 128
F32 = jnp.float32
BF16 = jnp.bfloat16


def split(value):
    high = value.astype(BF16)
    return high, (value - high.astype(F32)).astype(BF16)


def dot_nn(left, right):
    return lax.dot_general(left, right, (((1,), (0,)), ((), ())), preferred_element_type=F32)


def dot_nt(left, right):
    return lax.dot_general(left, right, (((1,), (1,)), ((), ())), preferred_element_type=F32)


def params(megabytes=12):
    return pltpu.CompilerParams(vmem_limit_bytes=megabytes * 1024 * 1024)


def project_kernel(x_ref, down_ref, up_ref, both_ref, square_ref):
    rank, features = down_ref.shape
    width = 1536
    down = jnp.zeros((rank, LANES), F32)
    up = jnp.zeros((rank, LANES), F32)
    total = jnp.zeros((LANES, LANES), F32)
    for start in range(0, features, width):
        rows = x_ref[:, start : start + width]
        down += dot_nt(down_ref[:, start : start + width], rows)
        up += dot_nt(up_ref[:, start : start + width], rows)
        wide = rows.astype(F32)
        for tile in range(0, wide.shape[1], LANES):
            part = wide[:, tile : tile + LANES]
            total += part * part
    both_ref[0:rank] = down
    both_ref[rank : 2 * rank] = up
    square_ref[...] = jnp.sum(total.T, axis=0, keepdims=True)


def project(rows, down, up):
    rank = down.shape[0]
    return pl.pallas_call(
        project_kernel,
        out_shape=[
            jax.ShapeDtypeStruct((2 * rank, LANES), F32),
            jax.ShapeDtypeStruct((1, LANES), F32),
        ],
        compiler_params=params(),
    )(rows, down, up)


def pair_kernel(own_ref, other_ref, share_ref, out_ref, pad_ref):
    rank, features = own_ref.shape
    members = out_ref.shape[0]
    pad_ref[...] = jnp.zeros_like(pad_ref)
    pad_ref[:, 0:rank] = dot_nt(own_ref[...], other_ref[...])
    packed = pad_ref[0:8]
    for group in range(1, rank // 8):
        packed += pltpu.roll(pad_ref[8 * group : 8 * group + 8], rank * group, 1)
    head = jnp.concatenate([packed, jnp.zeros_like(packed)], axis=0)
    tiles = features // members // LANES
    for member in range(members):
        parts = [head]
        for tile in range(member * tiles, (member + 1) * tiles):
            parts.append(share_ref[:, tile * LANES : (tile + 1) * LANES].astype(F32))
        out_ref[member] = jnp.concatenate(parts, axis=0).astype(BF16)


def pair_products(own, other, share, members):
    rank, features = own.shape
    rows = 16 + 8 * (features // members // LANES)
    return pl.pallas_call(
        pair_kernel,
        out_shape=jax.ShapeDtypeStruct((members, rows, LANES), BF16),
        scratch_shapes=[pltpu.VMEM((rank, LANES), F32)],
        compiler_params=params(),
    )(own, other, share)


def partner(position, member, sections):
    return position ^ member ^ ((sections // 2 + sections // 4) * (position & 1))


def partner_of(position, member, sections):
    mixed = position ^ member
    return mixed ^ ((sections // 2 + sections // 4) * (mixed & 1))


def order_kernel(rank, blocks, in_ref, both_ref, weight_ref, out_ref, share_ref, work_ref):
    position = lax.axis_index("section")
    lane = lax.broadcasted_iota(jnp.int32, (8, LANES), 1)
    tiles = rank * blocks // LANES
    pieces = [in_ref[partner(position, t, blocks)].astype(F32)[0:8] for t in range(blocks)]
    bands = []
    for member in range(in_ref.shape[0]):
        piece = in_ref[member].astype(F32)
        band = [piece[row : row + 8] for row in range(16, piece.shape[0], 8)]
        bands.append(jnp.concatenate(band, axis=1))
    rows = 8 * in_ref.shape[0]
    share_ref[0:rows] = jnp.concatenate(bands, axis=0).astype(BF16)
    share_ref[rows:] = weight_ref[...]
    for group in range(rank // 8):
        turned = [pltpu.roll(pieces[t], (rank * (t - group)) % LANES, 1) for t in range(blocks)]
        for tile in range(tiles):
            place = (lane + tile * LANES) // rank
            value = jnp.zeros((8, LANES), F32)
            for t in range(blocks):
                if rank * t < (tile + 1) * LANES and rank * (t + 1) > tile * LANES:
                    value = jnp.where(place == t, turned[t], value)
            work_ref[tile * rank + 8 * group : tile * rank + 8 * group + 8] = value
    work_ref[tiles * rank : (tiles + 2) * rank] = both_ref[...]
    filled = (tiles + 2) * rank
    if filled < work_ref.shape[0]:
        work_ref[filled:] = jnp.zeros((work_ref.shape[0] - filled, LANES), F32)
    payload = work_ref[...].astype(BF16)
    for copy in range(out_ref.shape[0]):
        out_ref[copy] = payload


def order_blocks(gathered, both, weight, rank, copies):
    blocks = gathered.shape[0]

    def kernel(*refs):
        order_kernel(rank, blocks, *refs)

    rows = -(-(rank * blocks // LANES + 2) * rank // 16) * 16
    members, height = gathered.shape[:2]
    return pl.pallas_call(
        kernel,
        out_shape=[
            jax.ShapeDtypeStruct((copies, rows, LANES), BF16),
            jax.ShapeDtypeStruct((8 * members + 2 * rank, (height - 16) // 8 * LANES), BF16),
        ],
        scratch_shapes=[pltpu.VMEM((rows, LANES), F32)],
        compiler_params=params(),
    )(gathered, both, weight)


def chain_kernel(rank, blocks, features, normalizer, grid_ref, square_ref, out_ref, *rest):
    plain_ref, turned_ref, act_ref, scaled_ref, grad_ref, skip_ref = rest
    size = rank * blocks
    tiles = size // LANES
    received = [grid_ref[b].astype(F32) for b in range(blocks)]
    whole = jnp.concatenate(
        [
            jnp.concatenate(
                [piece[tile * rank : (tile + 1) * rank] for tile in range(tiles)], axis=1
            )
            for piece in received
        ],
        axis=0,
    )
    plain_ref[...] = whole.astype(BF16)
    turned_ref[...] = whole.T.astype(BF16)

    def span(b):
        first = rank * b // LANES
        last = (rank * b + rank - 1) // LANES
        return first, last

    def columns(ref, b, start, stop):
        first, last = span(b)
        return ref[start:stop, first * LANES : (last + 1) * LANES]

    def placed(b, value):
        first, last = span(b)
        before = rank * b - first * LANES
        after = (last + 1) * LANES - rank * (b + 1)
        parts = []
        if before:
            parts.append(jnp.zeros((before, LANES), F32))
        parts.append(value)
        if after:
            parts.append(jnp.zeros((after, LANES), F32))
        return jnp.concatenate(parts, axis=0).astype(BF16)

    narrow, hidden = [], []
    for piece in received:
        narrow.append(piece[tiles * rank : (tiles + 1) * rank])
        hidden.append(piece[(tiles + 1) * rank : (tiles + 2) * rank])
    initial = list(hidden)
    square = square_ref[...]
    inverses, acts, pres, slopes, ends = [], [], [], [], []
    for b in range(blocks):
        inverse = lax.rsqrt(square / features + EPS)
        pre = narrow[b] * inverse
        sigmoid = 1.0 / (1.0 + jnp.exp(-pre))
        act = (pre * sigmoid).astype(BF16).astype(F32)
        act_ref[rank * b : rank * (b + 1)] = act
        inverses.append(inverse)
        acts.append(act)
        pres.append(pre)
        slopes.append(sigmoid * (1.0 + pre * (1.0 - sigmoid)))
        right = placed(b, act)
        if b + 1 < blocks:
            start = rank * (b + 1) // 16 * 16
            update = dot_nn(columns(turned_ref, b, start, size), right)
            for k in range(b + 1, blocks):
                narrow[k] = narrow[k] + update[rank * k - start : rank * (k + 1) - start]
        start = rank * b // 16 * 16
        update = dot_nn(columns(plain_ref, b, start, size), right)
        own = update[rank * b - start : rank * (b + 1) - start]
        for k in range(b + 1, blocks):
            hidden[k] = hidden[k] + update[rank * k - start : rank * (k + 1) - start]
        square = square + jnp.sum(act * (2.0 * hidden[b] + own), axis=0, keepdims=True)
        ends.append(hidden[b] + own)

    back = [jnp.zeros((rank, LANES), F32) for _ in range(blocks)]
    decay = jnp.zeros((1, LANES), F32)
    for k in reversed(range(blocks)):
        weight = 1.0 / normalizer - decay
        scaled = acts[k] * weight
        scaled_ref[rank * k : rank * (k + 1)] = scaled
        skip_ref[rank * k : rank * (k + 1)] = -decay * acts[k]
        incoming = ends[k] * weight - initial[k] / normalizer + back[k]
        grad = (incoming * slopes[k] * inverses[k]).astype(BF16).astype(F32)
        grad_ref[rank * k : rank * (k + 1)] = grad
        decay = decay + inverses[k] / features * jnp.sum(grad * pres[k], axis=0, keepdims=True)
        if k:
            stop = -(-rank * k // 16) * 16
            coarse = scaled.astype(BF16).astype(F32)
            fine = scaled - coarse
            update = (
                dot_nn(columns(turned_ref, k, 0, stop), placed(k, coarse))
                + dot_nn(columns(turned_ref, k, 0, stop), placed(k, fine))
                + dot_nn(columns(plain_ref, k, 0, stop), placed(k, grad))
            )
            for b in range(k):
                back[b] = back[b] + update[rank * b : rank * (b + 1)]

    position = lax.axis_index("section")
    mine = pl.ds(pl.multiple_of(position * rank, 8), rank)
    own_act = act_ref[mine].astype(BF16)
    own_high, own_low = split(scaled_ref[mine])
    own_grad = grad_ref[mine].astype(BF16)
    all_act = act_ref[...].astype(BF16)
    all_high, all_low = split(scaled_ref[...])
    all_grad = grad_ref[...].astype(BF16)
    place = lax.broadcasted_iota(jnp.int32, (rank, size), 1) // rank
    later = dot_nt(own_act, all_high) + dot_nt(own_act, all_low)
    earlier = dot_nt(own_high, all_act) + dot_nt(own_low, all_act)
    both_up = jnp.where(place >= position, later, earlier)
    crossed = jnp.where(
        place < position,
        dot_nt(own_grad, all_act),
        jnp.where(place > position, dot_nt(own_act, all_grad), 0.0),
    )
    groups = LANES // 8
    source = lax.broadcasted_iota(jnp.int32, (LANES, LANES), 0)
    target = lax.broadcasted_iota(jnp.int32, (LANES, LANES), 1)
    moved = source == target ^ (position * (LANES // groups))
    rows = jnp.concatenate([grad_ref[mine], skip_ref[mine]], axis=0).astype(BF16)
    rows = dot_nn(rows, jnp.where(moved, 1.0, 0.0).astype(BF16))
    source = lax.broadcasted_iota(jnp.int32, (size, size), 0)
    target = lax.broadcasted_iota(jnp.int32, (size, size), 1)
    block = target // rank
    moved = source == target + rank * ((block ^ position) - block)
    sums = jnp.concatenate([both_up, crossed], axis=0).astype(BF16)
    sums = dot_nn(sums, jnp.where(moved, 1.0, 0.0).astype(BF16))
    pieces = [rows]
    for value in (sums[0:rank], sums[rank : 2 * rank]):
        pieces += [value[:, tile * LANES : (tile + 1) * LANES] for tile in range(tiles)]
    payload = jnp.concatenate(pieces, axis=0).astype(BF16)
    for copy in range(out_ref.shape[0]):
        out_ref[copy] = payload


def run_chain(grid, square, rank, features, normalizer, copies):
    blocks = grid.shape[0]
    size = rank * blocks
    rows = 2 * rank + 2 * (size // LANES) * rank

    def kernel(*refs):
        chain_kernel(rank, blocks, features, normalizer, *refs)

    narrow = pltpu.VMEM((size, LANES), F32)
    square_matrix = pltpu.VMEM((size, size), BF16)
    return pl.pallas_call(
        kernel,
        out_shape=jax.ShapeDtypeStruct((copies, rows, LANES), BF16),
        scratch_shapes=[square_matrix, square_matrix, narrow, narrow, narrow, narrow],
        compiler_params=params(),
    )(grid, square)


def finish_kernel(rank, blocks, parts_ref, *refs):
    down_ref, up_ref, held_ref, copied = refs[blocks:]
    copies = [
        pltpu.make_async_copy(ref, held_ref.at[i], copied.at[i])
        for i, ref in enumerate(refs[:blocks])
    ]
    for copy in copies:
        copy.start()
    size = rank * blocks
    tiles = size // LANES
    members = parts_ref.shape[0]
    position = lax.axis_index("section")
    total = None
    left = []
    for member in range(members):
        piece = parts_ref[member]
        piece = piece.astype(F32)
        left.append(piece[0 : 2 * rank])
        sums = piece[2 * rank :]
        total = sums if total is None else total + sums

    lane = lax.broadcasted_iota(jnp.int32, (2 * rank, LANES), 1)
    width = LANES // members
    stride = 1
    while stride < members:
        upper = (lane // width) & stride != 0
        for low in range(members):
            if low & stride == 0:
                first, second = left[low], left[low | stride]
                left[low] = jnp.where(upper, pltpu.roll(second, stride * width, 1), first)
                left[low | stride] = jnp.where(
                    upper, second, pltpu.roll(first, LANES - stride * width, 1)
                )
        stride *= 2

    def unfold(first):
        return jnp.concatenate(
            [total[(first + tile) * rank : (first + tile + 1) * rank] for tile in range(tiles)], axis=1
        )

    both_up, crossed = unfold(0), unfold(tiles)
    place = (lax.broadcasted_iota(jnp.int32, (rank, size), 1) // rank) ^ position
    below = jnp.where(place < position, crossed, 0.0)
    above = jnp.where(place > position, crossed, 0.0)
    rows = 8 * members
    result = jnp.zeros((2 * rank, held_ref.shape[2]), F32)
    weights = []
    for i in range(blocks):
        copies[i].wait()
        result += dot_nn(left[i].astype(BF16), held_ref[i, 0:rows])
        weights.append(held_ref[i, rows:].astype(F32))
    all_down = jnp.concatenate([w[0:rank] for w in weights], axis=0).astype(BF16)
    all_up = jnp.concatenate([w[rank : 2 * rank] for w in weights], axis=0).astype(BF16)
    high, low = split(jnp.concatenate([below, both_up], axis=0))
    result += dot_nn(high, all_up) + dot_nn(low, all_up)
    high, low = split(above)
    cross = dot_nn(high, all_down) + dot_nn(low, all_down)
    down_ref[0] = result[0:rank]
    up_ref[0] = result[rank : 2 * rank] + cross


def finish(parts, slices, rank):
    blocks = len(slices)
    width = slices[0].shape[1]

    def kernel(*refs):
        finish_kernel(rank, blocks, *refs)

    shape = jax.ShapeDtypeStruct((1, rank, width), F32)
    vmem = pl.BlockSpec(memory_space=pltpu.VMEM)
    return pl.pallas_call(
        kernel,
        in_specs=[vmem] + [pl.BlockSpec(memory_space=pl.ANY)] * blocks,
        out_specs=[vmem, vmem],
        out_shape=[shape, shape],
        scratch_shapes=[
            pltpu.VMEM((blocks,) + slices[0].shape, BF16),
            pltpu.SemaphoreType.DMA((blocks,)),
        ],
        compiler_params=params(60),
    )(parts, *slices)


def swapped(value, distance, count):
    return lax.ppermute(value, "section", [(i, i ^ distance) for i in range(count)])


def shards(inputs, down_proj, up_proj):
    sections = lax.axis_size("section")
    members = lax.axis_size("dp")
    position = lax.axis_index("section")
    member = lax.axis_index("dp")
    own_down, own_up = down_proj[0], up_proj[0]
    rank, features = own_down.shape
    width = features // members
    pipes, micro, count = inputs.shape[:3]
    normalizer = float(micro * count * members)
    all_rows = inputs.reshape(pipes * micro * count, features)

    route = [
        (partner(s, d, sections) * members + d, s * members + d)
        for s in range(sections)
        for d in range(members)
    ]
    receiver = partner_of(position, member, sections)
    outgoing = jnp.where(receiver >= position, own_up, own_down)
    other = lax.ppermute(outgoing, ("section", "dp"), route)

    share = lax.dynamic_index_in_dim(
        inputs.reshape(sections, count, features), position, 0, keepdims=False
    )
    weight = jnp.concatenate(
        [lax.dynamic_slice_in_dim(w, member * width, width, 1) for w in (own_down, own_up)], axis=0
    )
    both, square = project(all_rows, own_down, own_up)
    other, share, weight, both, square = lax.optimization_barrier(
        (other, share, weight, both, square)
    )

    products = lax.all_to_all(pair_products(own_up, other, share, members), "dp", 0, 0)
    grid, share = order_blocks(products, both, weight, rank, sections)
    grid = lax.all_to_all(grid, "section", 0, 0)
    grid, share = lax.optimization_barrier((grid, share))

    half = sections // 2
    slices = {0: share}
    for distance in (2, half - 2, half, *range(4, half - 2, 2)):
        slices[distance] = swapped(share, distance, sections)
    parts = run_chain(grid, square, rank, features, normalizer, members)
    parts, slices = lax.optimization_barrier((parts, slices))
    for distance in range(2, half, 2):
        slices[half + distance] = swapped(slices[half], distance, sections)
    for distance in range(0, sections, 2):
        slices[distance + 1] = swapped(slices[distance], 1, sections)
    parts = lax.all_to_all(parts, "dp", 0, 0)
    return finish(parts, [slices[d] for d in range(sections)], rank)


def solution(mesh):
    placed = (P(None, None, "dp", None), P("section", None, None), P("section", None, None))
    return jax.shard_map(
        shards,
        mesh=mesh,
        in_specs=placed,
        out_specs=(P("section", None, "dp"), P("section", None, "dp")),
        check_vma=False,
    )
```

```python
import jax
import jax.numpy as jnp
from jax import lax
from jax.experimental import pallas as pl
from jax.experimental.pallas import tpu as pltpu
from jax.sharding import PartitionSpec as P

EPS = 1e-05
LANES = 128
F32 = jnp.float32
BF16 = jnp.bfloat16


def split(value):
    high = value.astype(BF16)
    return high, (value - high.astype(F32)).astype(BF16)


def dot_nn(left, right):
    return lax.dot_general(left, right, (((1,), (0,)), ((), ())), preferred_element_type=F32)


def dot_nt(left, right):
    return lax.dot_general(left, right, (((1,), (1,)), ((), ())), preferred_element_type=F32)


def params(megabytes=12):
    return pltpu.CompilerParams(vmem_limit_bytes=megabytes * 1024 * 1024)


def project_kernel(x_ref, down_ref, up_ref, both_ref, square_ref):
    rank, features = down_ref.shape
    width = 1536
    down = jnp.zeros((rank, LANES), F32)
    up = jnp.zeros((rank, LANES), F32)
    total = jnp.zeros((LANES, LANES), F32)
    for start in range(0, features, width):
        rows = x_ref[:, start : start + width]
        down += dot_nt(down_ref[:, start : start + width], rows)
        up += dot_nt(up_ref[:, start : start + width], rows)
        wide = rows.astype(F32)
        for tile in range(0, wide.shape[1], LANES):
            part = wide[:, tile : tile + LANES]
            total += part * part
    both_ref[0:rank] = down
    both_ref[rank : 2 * rank] = up
    square_ref[...] = jnp.sum(total.T, axis=0, keepdims=True)


def project(rows, down, up):
    rank = down.shape[0]
    return pl.pallas_call(
        project_kernel,
        out_shape=[
            jax.ShapeDtypeStruct((2 * rank, LANES), F32),
            jax.ShapeDtypeStruct((1, LANES), F32),
        ],
        compiler_params=params(),
    )(rows, down, up)


def pair_kernel(own_ref, other_ref, share_ref, out_ref, pad_ref):
    rank, features = own_ref.shape
    members = out_ref.shape[0]
    pad_ref[...] = jnp.zeros_like(pad_ref)
    pad_ref[:, 0:rank] = dot_nt(own_ref[...], other_ref[...])
    packed = pad_ref[0:8]
    for group in range(1, rank // 8):
        packed += pltpu.roll(pad_ref[8 * group : 8 * group + 8], rank * group, 1)
    head = jnp.concatenate([packed, jnp.zeros_like(packed)], axis=0)
    tiles = features // members // LANES
    for member in range(members):
        parts = [head]
        for tile in range(member * tiles, (member + 1) * tiles):
            parts.append(share_ref[:, tile * LANES : (tile + 1) * LANES].astype(F32))
        out_ref[member] = jnp.concatenate(parts, axis=0).astype(BF16)


def pair_products(own, other, share, members):
    rank, features = own.shape
    rows = 16 + 8 * (features // members // LANES)
    return pl.pallas_call(
        pair_kernel,
        out_shape=jax.ShapeDtypeStruct((members, rows, LANES), BF16),
        scratch_shapes=[pltpu.VMEM((rank, LANES), F32)],
        compiler_params=params(),
    )(own, other, share)


def partner(position, member, sections):
    return position ^ member ^ ((sections // 2 + sections // 4) * (position & 1))


def partner_of(position, member, sections):
    mixed = position ^ member
    return mixed ^ ((sections // 2 + sections // 4) * (mixed & 1))


def order_kernel(rank, blocks, in_ref, both_ref, weight_ref, out_ref, share_ref, work_ref):
    position = lax.axis_index("section")
    lane = lax.broadcasted_iota(jnp.int32, (8, LANES), 1)
    tiles = rank * blocks // LANES
    pieces = [in_ref[partner(position, t, blocks)].astype(F32)[0:8] for t in range(blocks)]
    bands = []
    for member in range(in_ref.shape[0]):
        piece = in_ref[member].astype(F32)
        band = [piece[row : row + 8] for row in range(16, piece.shape[0], 8)]
        bands.append(jnp.concatenate(band, axis=1))
    rows = 8 * in_ref.shape[0]
    share_ref[0:rows] = jnp.concatenate(bands, axis=0).astype(BF16)
    share_ref[rows:] = weight_ref[...]
    for group in range(rank // 8):
        turned = [pltpu.roll(pieces[t], (rank * (t - group)) % LANES, 1) for t in range(blocks)]
        for tile in range(tiles):
            place = (lane + tile * LANES) // rank
            value = jnp.zeros((8, LANES), F32)
            for t in range(blocks):
                if rank * t < (tile + 1) * LANES and rank * (t + 1) > tile * LANES:
                    value = jnp.where(place == t, turned[t], value)
            work_ref[tile * rank + 8 * group : tile * rank + 8 * group + 8] = value
    work_ref[tiles * rank : (tiles + 2) * rank] = both_ref[...]
    filled = (tiles + 2) * rank
    if filled < work_ref.shape[0]:
        work_ref[filled:] = jnp.zeros((work_ref.shape[0] - filled, LANES), F32)
    payload = work_ref[...].astype(BF16)
    for copy in range(out_ref.shape[0]):
        out_ref[copy] = payload


def order_blocks(gathered, both, weight, rank, copies):
    blocks = gathered.shape[0]

    def kernel(*refs):
        order_kernel(rank, blocks, *refs)

    rows = -(-(rank * blocks // LANES + 2) * rank // 16) * 16
    members, height = gathered.shape[:2]
    return pl.pallas_call(
        kernel,
        out_shape=[
            jax.ShapeDtypeStruct((copies, rows, LANES), BF16),
            jax.ShapeDtypeStruct((8 * members + 2 * rank, (height - 16) // 8 * LANES), BF16),
        ],
        scratch_shapes=[pltpu.VMEM((rows, LANES), F32)],
        compiler_params=params(),
    )(gathered, both, weight)


def chain_kernel(rank, blocks, features, normalizer, grid_ref, square_ref, out_ref, *rest):
    plain_ref, turned_ref, act_ref, scaled_ref, grad_ref, skip_ref = rest
    size = rank * blocks
    tiles = size // LANES
    received = [grid_ref[b].astype(F32) for b in range(blocks)]
    whole = jnp.concatenate(
        [
            jnp.concatenate(
                [piece[tile * rank : (tile + 1) * rank] for tile in range(tiles)], axis=1
            )
            for piece in received
        ],
        axis=0,
    )
    plain_ref[...] = whole.astype(BF16)
    turned_ref[...] = whole.T.astype(BF16)

    def span(b):
        first = rank * b // LANES
        last = (rank * b + rank - 1) // LANES
        return first, last

    def columns(ref, b, start, stop):
        first, last = span(b)
        return ref[start:stop, first * LANES : (last + 1) * LANES]

    def placed(b, value):
        first, last = span(b)
        before = rank * b - first * LANES
        after = (last + 1) * LANES - rank * (b + 1)
        parts = []
        if before:
            parts.append(jnp.zeros((before, LANES), F32))
        parts.append(value)
        if after:
            parts.append(jnp.zeros((after, LANES), F32))
        return jnp.concatenate(parts, axis=0).astype(BF16)

    narrow, hidden = [], []
    for piece in received:
        narrow.append(piece[tiles * rank : (tiles + 1) * rank])
        hidden.append(piece[(tiles + 1) * rank : (tiles + 2) * rank])
    initial = list(hidden)
    square = square_ref[...]
    inverses, acts, pres, slopes, ends = [], [], [], [], []
    for b in range(blocks):
        inverse = lax.rsqrt(square / features + EPS)
        pre = narrow[b] * inverse
        sigmoid = 1.0 / (1.0 + jnp.exp(-pre))
        act = (pre * sigmoid).astype(BF16).astype(F32)
        act_ref[rank * b : rank * (b + 1)] = act
        inverses.append(inverse)
        acts.append(act)
        pres.append(pre)
        slopes.append(sigmoid * (1.0 + pre * (1.0 - sigmoid)))
        right = placed(b, act)
        if b + 1 < blocks:
            start = rank * (b + 1) // 16 * 16
            update = dot_nn(columns(turned_ref, b, start, size), right)
            for k in range(b + 1, blocks):
                narrow[k] = narrow[k] + update[rank * k - start : rank * (k + 1) - start]
        start = rank * b // 16 * 16
        update = dot_nn(columns(plain_ref, b, start, size), right)
        own = update[rank * b - start : rank * (b + 1) - start]
        for k in range(b + 1, blocks):
            hidden[k] = hidden[k] + update[rank * k - start : rank * (k + 1) - start]
        square = square + jnp.sum(act * (2.0 * hidden[b] + own), axis=0, keepdims=True)
        ends.append(hidden[b] + own)

    back = [jnp.zeros((rank, LANES), F32) for _ in range(blocks)]
    decay = jnp.zeros((1, LANES), F32)
    for k in reversed(range(blocks)):
        weight = 1.0 / normalizer - decay
        scaled = acts[k] * weight
        scaled_ref[rank * k : rank * (k + 1)] = scaled
        skip_ref[rank * k : rank * (k + 1)] = -decay * acts[k]
        incoming = ends[k] * weight - initial[k] / normalizer + back[k]
        grad = (incoming * slopes[k] * inverses[k]).astype(BF16).astype(F32)
        grad_ref[rank * k : rank * (k + 1)] = grad
        decay = decay + inverses[k] / features * jnp.sum(grad * pres[k], axis=0, keepdims=True)
        if k:
            stop = -(-rank * k // 16) * 16
            coarse = scaled.astype(BF16).astype(F32)
            fine = scaled - coarse
            update = (
                dot_nn(columns(turned_ref, k, 0, stop), placed(k, coarse))
                + dot_nn(columns(turned_ref, k, 0, stop), placed(k, fine))
                + dot_nn(columns(plain_ref, k, 0, stop), placed(k, grad))
            )
            for b in range(k):
                back[b] = back[b] + update[rank * b : rank * (b + 1)]

    position = lax.axis_index("section")
    mine = pl.ds(pl.multiple_of(position * rank, 8), rank)
    own_act = act_ref[mine].astype(BF16)
    own_high, own_low = split(scaled_ref[mine])
    own_grad = grad_ref[mine].astype(BF16)
    all_act = act_ref[...].astype(BF16)
    all_high, all_low = split(scaled_ref[...])
    all_grad = grad_ref[...].astype(BF16)
    place = lax.broadcasted_iota(jnp.int32, (rank, size), 1) // rank
    later = dot_nt(own_act, all_high) + dot_nt(own_act, all_low)
    earlier = dot_nt(own_high, all_act) + dot_nt(own_low, all_act)
    both_up = jnp.where(place >= position, later, earlier)
    crossed = jnp.where(
        place < position,
        dot_nt(own_grad, all_act),
        jnp.where(place > position, dot_nt(own_act, all_grad), 0.0),
    )
    groups = LANES // 8
    source = lax.broadcasted_iota(jnp.int32, (LANES, LANES), 0)
    target = lax.broadcasted_iota(jnp.int32, (LANES, LANES), 1)
    moved = source == target ^ (position * (LANES // groups))
    rows = jnp.concatenate([grad_ref[mine], skip_ref[mine]], axis=0).astype(BF16)
    rows = dot_nn(rows, jnp.where(moved, 1.0, 0.0).astype(BF16))
    source = lax.broadcasted_iota(jnp.int32, (size, size), 0)
    target = lax.broadcasted_iota(jnp.int32, (size, size), 1)
    block = target // rank
    moved = source == target + rank * ((block ^ position) - block)
    sums = jnp.concatenate([both_up, crossed], axis=0).astype(BF16)
    sums = dot_nn(sums, jnp.where(moved, 1.0, 0.0).astype(BF16))
    pieces = [rows]
    for value in (sums[0:rank], sums[rank : 2 * rank]):
        pieces += [value[:, tile * LANES : (tile + 1) * LANES] for tile in range(tiles)]
    out_ref[...] = jnp.concatenate(pieces, axis=0).astype(BF16)


def run_chain(grid, square, rank, features, normalizer):
    blocks = grid.shape[0]
    size = rank * blocks
    rows = 2 * rank + 2 * (size // LANES) * rank

    def kernel(*refs):
        chain_kernel(rank, blocks, features, normalizer, *refs)

    narrow = pltpu.VMEM((size, LANES), F32)
    square_matrix = pltpu.VMEM((size, size), BF16)
    return pl.pallas_call(
        kernel,
        out_shape=jax.ShapeDtypeStruct((rows, LANES), BF16),
        scratch_shapes=[square_matrix, square_matrix, narrow, narrow, narrow, narrow],
        compiler_params=params(),
    )(grid, square)


def combine_kernel(rank, own_ref, other_ref, out_ref):
    own, other = own_ref[...], other_ref[...]
    both = own.astype(F32) + other.astype(F32)
    payload = jnp.concatenate(
        [own[0 : 2 * rank], other[0 : 2 * rank], both[2 * rank :].astype(BF16)], axis=0
    )
    for copy in range(out_ref.shape[0]):
        out_ref[copy] = payload


def combine(own, other, rank, copies):
    def kernel(*refs):
        combine_kernel(rank, *refs)

    rows = own.shape[0] + 2 * rank
    return pl.pallas_call(
        kernel,
        out_shape=jax.ShapeDtypeStruct((copies, rows, LANES), BF16),
        compiler_params=params(),
    )(own, other)


def finish_kernel(rank, blocks, parts_ref, *refs):
    down_ref, up_ref, held_ref, copied = refs[blocks:]
    copies = [
        pltpu.make_async_copy(ref, held_ref.at[i], copied.at[i])
        for i, ref in enumerate(refs[:blocks])
    ]
    for copy in copies:
        copy.start()
    size = rank * blocks
    tiles = size // LANES
    near = parts_ref.shape[0]
    position = lax.axis_index("section")
    own_half = lax.axis_index("dp") // near
    total = parts_ref[0, 4 * rank :].astype(F32)
    for member in range(1, near):
        total += parts_ref[member, 4 * rank :].astype(F32)

    def unfold(first):
        return jnp.concatenate(
            [total[(first + tile) * rank : (first + tile + 1) * rank] for tile in range(tiles)], axis=1
        )

    both_up, crossed = unfold(0), unfold(tiles)
    place = (lax.broadcasted_iota(jnp.int32, (rank, size), 1) // rank) ^ position
    below = jnp.where(place < position, crossed, 0.0)
    above = jnp.where(place > position, crossed, 0.0)
    for copy in copies:
        copy.wait()
    wide = [held_ref[i].astype(F32) for i in range(blocks)]

    def stacked(first, count):
        return jnp.concatenate([piece[first : first + count] for piece in wide], axis=0).astype(BF16)

    result = jnp.zeros((2 * rank, held_ref.shape[2]), F32)
    for half in range(2):
        start = pl.multiple_of((own_half ^ half) * 2 * rank, 16)
        for member in range(near):
            left = parts_ref[member, pl.ds(start, 2 * rank)]
            result += dot_nn(left, stacked(8 * (half * near + member), 8))
    rows = 16 * near
    all_down = stacked(rows, rank)
    all_up = stacked(rows + rank, rank)
    high, low = split(jnp.concatenate([below, both_up], axis=0))
    result += dot_nn(high, all_up) + dot_nn(low, all_up)
    high, low = split(above)
    cross = dot_nn(high, all_down) + dot_nn(low, all_down)
    down_ref[0] = result[0:rank]
    up_ref[0] = result[rank : 2 * rank] + cross


def finish(parts, slices, rank):
    blocks = len(slices)
    width = slices[0].shape[1]

    def kernel(*refs):
        finish_kernel(rank, blocks, *refs)

    shape = jax.ShapeDtypeStruct((1, rank, width), F32)
    vmem = pl.BlockSpec(memory_space=pltpu.VMEM)
    return pl.pallas_call(
        kernel,
        in_specs=[vmem] + [pl.BlockSpec(memory_space=pl.ANY)] * blocks,
        out_specs=[vmem, vmem],
        out_shape=[shape, shape],
        scratch_shapes=[
            pltpu.VMEM((blocks,) + slices[0].shape, BF16),
            pltpu.SemaphoreType.DMA((blocks,)),
        ],
        compiler_params=params(60),
    )(parts, *slices)


def moved(value, axis, distance, count):
    return lax.ppermute(value, axis, [(i, i ^ distance) for i in range(count)])


def swapped(value, distance, count):
    return moved(value, "section", distance, count)


def shards(inputs, down_proj, up_proj):
    sections = lax.axis_size("section")
    members = lax.axis_size("dp")
    position = lax.axis_index("section")
    member = lax.axis_index("dp")
    own_down, own_up = down_proj[0], up_proj[0]
    rank, features = own_down.shape
    width = features // members
    pipes, micro, count = inputs.shape[:3]
    normalizer = float(micro * count * members)
    all_rows = inputs.reshape(pipes * micro * count, features)

    route = [
        (partner(s, d, sections) * members + d, s * members + d)
        for s in range(sections)
        for d in range(members)
    ]
    receiver = partner_of(position, member, sections)
    outgoing = jnp.where(receiver >= position, own_up, own_down)
    other = lax.ppermute(outgoing, ("section", "dp"), route)

    share = lax.dynamic_index_in_dim(
        inputs.reshape(sections, count, features), position, 0, keepdims=False
    )
    weight = jnp.concatenate(
        [lax.dynamic_slice_in_dim(w, member * width, width, 1) for w in (own_down, own_up)], axis=0
    )
    both, square = project(all_rows, own_down, own_up)
    other, share, weight, both, square = lax.optimization_barrier(
        (other, share, weight, both, square)
    )

    products = lax.all_to_all(pair_products(own_up, other, share, members), "dp", 0, 0)
    grid, share = order_blocks(products, both, weight, rank, sections)
    grid = lax.all_to_all(grid, "section", 0, 0)

    half = sections // 2
    slices = {0: share}
    for distance in (2, half - 2, half):
        slices[distance] = swapped(share, distance, sections)
    parts = run_chain(grid, square, rank, features, normalizer)
    parts, slices = lax.optimization_barrier((parts, slices))
    for distance in range(4, half - 2, 2):
        slices[distance] = swapped(share, distance, sections)
    last = half - 2
    slices[half + last] = swapped(slices[half], last, sections)
    for distance in range(2, last, 2):
        slices[half + distance] = swapped(slices[distance], half, sections)
    for distance in range(0, sections, 2):
        slices[distance + 1] = swapped(slices[distance], 1, sections)
    line = members // 2
    parts = combine(parts, moved(parts, "dp", line, members), rank, line)
    groups = [list(range(start, start + line)) for start in (0, line)]
    parts = lax.all_to_all(parts, "dp", 0, 0, axis_index_groups=groups)
    return finish(parts, [slices[d] for d in range(sections)], rank)


def solution(mesh):
    placed = (P(None, None, "dp", None), P("section", None, None), P("section", None, None))
    return jax.shard_map(
        shards,
        mesh=mesh,
        in_specs=placed,
        out_specs=(P("section", None, "dp"), P("section", None, "dp")),
        check_vma=False,
    )
```

```python
import jax
import jax.numpy as jnp
from jax import lax
from jax.experimental import pallas as pl
from jax.experimental.pallas import tpu as pltpu
from jax.sharding import PartitionSpec as P

EPS = 1e-05
LANES = 128
F32 = jnp.float32
BF16 = jnp.bfloat16


def split(value):
    high = value.astype(BF16)
    return high, (value - high.astype(F32)).astype(BF16)


def dot_nn(left, right):
    return lax.dot_general(left, right, (((1,), (0,)), ((), ())), preferred_element_type=F32)


def dot_nt(left, right):
    return lax.dot_general(left, right, (((1,), (1,)), ((), ())), preferred_element_type=F32)


def params(megabytes=12):
    return pltpu.CompilerParams(vmem_limit_bytes=megabytes * 1024 * 1024)


def project_kernel(x_ref, down_ref, up_ref, both_ref, square_ref):
    rank, features = down_ref.shape
    width = 1536
    down = jnp.zeros((rank, LANES), F32)
    up = jnp.zeros((rank, LANES), F32)
    total = jnp.zeros((LANES, LANES), F32)
    for start in range(0, features, width):
        rows = x_ref[:, start : start + width]
        down += dot_nt(down_ref[:, start : start + width], rows)
        up += dot_nt(up_ref[:, start : start + width], rows)
        wide = rows.astype(F32)
        for tile in range(0, wide.shape[1], LANES):
            part = wide[:, tile : tile + LANES]
            total += part * part
    both_ref[0:rank] = down
    both_ref[rank : 2 * rank] = up
    square_ref[...] = jnp.sum(total.T, axis=0, keepdims=True)


def project(rows, down, up):
    rank = down.shape[0]
    return pl.pallas_call(
        project_kernel,
        out_shape=[
            jax.ShapeDtypeStruct((2 * rank, LANES), F32),
            jax.ShapeDtypeStruct((1, LANES), F32),
        ],
        compiler_params=params(),
    )(rows, down, up)


def pair_kernel(own_ref, other_ref, share_ref, out_ref, pad_ref):
    rank, features = own_ref.shape
    members = out_ref.shape[0]
    pad_ref[...] = jnp.zeros_like(pad_ref)
    pad_ref[:, 0:rank] = dot_nt(own_ref[...], other_ref[...])
    packed = pad_ref[0:8]
    for group in range(1, rank // 8):
        packed += pltpu.roll(pad_ref[8 * group : 8 * group + 8], rank * group, 1)
    head = jnp.concatenate([packed, jnp.zeros_like(packed)], axis=0)
    tiles = features // members // LANES
    for member in range(members):
        parts = [head]
        for tile in range(member * tiles, (member + 1) * tiles):
            parts.append(share_ref[:, tile * LANES : (tile + 1) * LANES].astype(F32))
        out_ref[member] = jnp.concatenate(parts, axis=0).astype(BF16)


def pair_products(own, other, share, members):
    rank, features = own.shape
    rows = 16 + 8 * (features // members // LANES)
    return pl.pallas_call(
        pair_kernel,
        out_shape=jax.ShapeDtypeStruct((members, rows, LANES), BF16),
        scratch_shapes=[pltpu.VMEM((rank, LANES), F32)],
        compiler_params=params(),
    )(own, other, share)


def partner(position, member, sections):
    return position ^ member ^ ((sections // 2 + sections // 4) * (position & 1))


def partner_of(position, member, sections):
    mixed = position ^ member
    return mixed ^ ((sections // 2 + sections // 4) * (mixed & 1))


def order_kernel(rank, blocks, in_ref, both_ref, weight_ref, out_ref, share_ref, work_ref):
    position = lax.axis_index("section")
    lane = lax.broadcasted_iota(jnp.int32, (8, LANES), 1)
    tiles = rank * blocks // LANES
    pieces = [in_ref[partner(position, t, blocks)].astype(F32)[0:8] for t in range(blocks)]
    bands = []
    for member in range(in_ref.shape[0]):
        piece = in_ref[member].astype(F32)
        band = [piece[row : row + 8] for row in range(16, piece.shape[0], 8)]
        bands.append(jnp.concatenate(band, axis=1))
    rows = 8 * in_ref.shape[0]
    share_ref[0:rows] = jnp.concatenate(bands, axis=0).astype(BF16)
    share_ref[rows:] = weight_ref[...]
    for group in range(rank // 8):
        turned = [pltpu.roll(pieces[t], (rank * (t - group)) % LANES, 1) for t in range(blocks)]
        for tile in range(tiles):
            place = (lane + tile * LANES) // rank
            value = jnp.zeros((8, LANES), F32)
            for t in range(blocks):
                if rank * t < (tile + 1) * LANES and rank * (t + 1) > tile * LANES:
                    value = jnp.where(place == t, turned[t], value)
            work_ref[tile * rank + 8 * group : tile * rank + 8 * group + 8] = value
    work_ref[tiles * rank : (tiles + 2) * rank] = both_ref[...]
    filled = (tiles + 2) * rank
    if filled < work_ref.shape[0]:
        work_ref[filled:] = jnp.zeros((work_ref.shape[0] - filled, LANES), F32)
    payload = work_ref[...].astype(BF16)
    for copy in range(out_ref.shape[0]):
        out_ref[copy] = payload


def order_blocks(gathered, both, weight, rank, copies):
    blocks = gathered.shape[0]

    def kernel(*refs):
        order_kernel(rank, blocks, *refs)

    rows = -(-(rank * blocks // LANES + 2) * rank // 16) * 16
    members, height = gathered.shape[:2]
    return pl.pallas_call(
        kernel,
        out_shape=[
            jax.ShapeDtypeStruct((copies, rows, LANES), BF16),
            jax.ShapeDtypeStruct((8 * members + 2 * rank, (height - 16) // 8 * LANES), BF16),
        ],
        scratch_shapes=[pltpu.VMEM((rows, LANES), F32)],
        compiler_params=params(),
    )(gathered, both, weight)


def chain_kernel(rank, blocks, features, normalizer, grid_ref, square_ref, out_ref, *rest):
    plain_ref, turned_ref, act_ref, scaled_ref, grad_ref, skip_ref = rest
    size = rank * blocks
    tiles = size // LANES
    received = [grid_ref[b].astype(F32) for b in range(blocks)]
    whole = jnp.concatenate(
        [
            jnp.concatenate(
                [piece[tile * rank : (tile + 1) * rank] for tile in range(tiles)], axis=1
            )
            for piece in received
        ],
        axis=0,
    )
    plain_ref[...] = whole.astype(BF16)
    turned_ref[...] = whole.T.astype(BF16)

    def span(b):
        first = rank * b // LANES
        last = (rank * b + rank - 1) // LANES
        return first, last

    def columns(ref, b, start, stop):
        first, last = span(b)
        return ref[start:stop, first * LANES : (last + 1) * LANES]

    def placed(b, value):
        first, last = span(b)
        before = rank * b - first * LANES
        after = (last + 1) * LANES - rank * (b + 1)
        parts = []
        if before:
            parts.append(jnp.zeros((before, LANES), F32))
        parts.append(value)
        if after:
            parts.append(jnp.zeros((after, LANES), F32))
        return jnp.concatenate(parts, axis=0).astype(BF16)

    narrow, hidden = [], []
    for piece in received:
        narrow.append(piece[tiles * rank : (tiles + 1) * rank])
        hidden.append(piece[(tiles + 1) * rank : (tiles + 2) * rank])
    initial = list(hidden)
    square = square_ref[...]
    inverses, acts, pres, slopes, ends = [], [], [], [], []
    for b in range(blocks):
        inverse = lax.rsqrt(square / features + EPS)
        pre = narrow[b] * inverse
        sigmoid = 1.0 / (1.0 + jnp.exp(-pre))
        act = (pre * sigmoid).astype(BF16).astype(F32)
        act_ref[rank * b : rank * (b + 1)] = act
        inverses.append(inverse)
        acts.append(act)
        pres.append(pre)
        slopes.append(sigmoid * (1.0 + pre * (1.0 - sigmoid)))
        right = placed(b, act)
        if b + 1 < blocks:
            start = rank * (b + 1) // 16 * 16
            update = dot_nn(columns(turned_ref, b, start, size), right)
            for k in range(b + 1, blocks):
                narrow[k] = narrow[k] + update[rank * k - start : rank * (k + 1) - start]
        start = rank * b // 16 * 16
        update = dot_nn(columns(plain_ref, b, start, size), right)
        own = update[rank * b - start : rank * (b + 1) - start]
        for k in range(b + 1, blocks):
            hidden[k] = hidden[k] + update[rank * k - start : rank * (k + 1) - start]
        square = square + jnp.sum(act * (2.0 * hidden[b] + own), axis=0, keepdims=True)
        ends.append(hidden[b] + own)

    back = [jnp.zeros((rank, LANES), F32) for _ in range(blocks)]
    decay = jnp.zeros((1, LANES), F32)
    for k in reversed(range(blocks)):
        weight = 1.0 / normalizer - decay
        scaled = acts[k] * weight
        scaled_ref[rank * k : rank * (k + 1)] = scaled
        skip_ref[rank * k : rank * (k + 1)] = -decay * acts[k]
        incoming = ends[k] * weight - initial[k] / normalizer + back[k]
        grad = (incoming * slopes[k] * inverses[k]).astype(BF16).astype(F32)
        grad_ref[rank * k : rank * (k + 1)] = grad
        decay = decay + inverses[k] / features * jnp.sum(grad * pres[k], axis=0, keepdims=True)
        if k:
            stop = -(-rank * k // 16) * 16
            coarse = scaled.astype(BF16).astype(F32)
            fine = scaled - coarse
            update = (
                dot_nn(columns(turned_ref, k, 0, stop), placed(k, coarse))
                + dot_nn(columns(turned_ref, k, 0, stop), placed(k, fine))
                + dot_nn(columns(plain_ref, k, 0, stop), placed(k, grad))
            )
            for b in range(k):
                back[b] = back[b] + update[rank * b : rank * (b + 1)]

    position = lax.axis_index("section")
    mine = pl.ds(pl.multiple_of(position * rank, 8), rank)
    own_act = act_ref[mine].astype(BF16)
    own_high, own_low = split(scaled_ref[mine])
    own_grad = grad_ref[mine].astype(BF16)
    all_act = act_ref[...].astype(BF16)
    all_high, all_low = split(scaled_ref[...])
    all_grad = grad_ref[...].astype(BF16)
    place = lax.broadcasted_iota(jnp.int32, (rank, size), 1) // rank
    later = dot_nt(own_act, all_high) + dot_nt(own_act, all_low)
    earlier = dot_nt(own_high, all_act) + dot_nt(own_low, all_act)
    both_up = jnp.where(place >= position, later, earlier)
    crossed = jnp.where(
        place < position,
        dot_nt(own_grad, all_act),
        jnp.where(place > position, dot_nt(own_act, all_grad), 0.0),
    )
    groups = LANES // 8
    source = lax.broadcasted_iota(jnp.int32, (LANES, LANES), 0)
    target = lax.broadcasted_iota(jnp.int32, (LANES, LANES), 1)
    moved = source == target ^ (position * (LANES // groups))
    rows = jnp.concatenate([grad_ref[mine], skip_ref[mine]], axis=0).astype(BF16)
    rows = dot_nn(rows, jnp.where(moved, 1.0, 0.0).astype(BF16))
    source = lax.broadcasted_iota(jnp.int32, (size, size), 0)
    target = lax.broadcasted_iota(jnp.int32, (size, size), 1)
    block = target // rank
    moved = source == target + rank * ((block ^ position) - block)
    sums = jnp.concatenate([both_up, crossed], axis=0).astype(BF16)
    sums = dot_nn(sums, jnp.where(moved, 1.0, 0.0).astype(BF16))
    pieces = [rows]
    for value in (sums[0:rank], sums[rank : 2 * rank]):
        pieces += [value[:, tile * LANES : (tile + 1) * LANES] for tile in range(tiles)]
    out_ref[...] = jnp.concatenate(pieces, axis=0).astype(BF16)


def run_chain(grid, square, rank, features, normalizer):
    blocks = grid.shape[0]
    size = rank * blocks
    rows = 2 * rank + 2 * (size // LANES) * rank

    def kernel(*refs):
        chain_kernel(rank, blocks, features, normalizer, *refs)

    narrow = pltpu.VMEM((size, LANES), F32)
    square_matrix = pltpu.VMEM((size, size), BF16)
    return pl.pallas_call(
        kernel,
        out_shape=jax.ShapeDtypeStruct((rows, LANES), BF16),
        scratch_shapes=[square_matrix, square_matrix, narrow, narrow, narrow, narrow],
        compiler_params=params(),
    )(grid, square)


def combine_kernel(rank, own_ref, other_ref, out_ref):
    own, other = own_ref[...], other_ref[...]
    both = own.astype(F32) + other.astype(F32)
    payload = jnp.concatenate(
        [own[0 : 2 * rank], other[0 : 2 * rank], both[2 * rank :].astype(BF16)], axis=0
    )
    for copy in range(out_ref.shape[0]):
        out_ref[copy] = payload


def combine(own, other, rank, copies):
    def kernel(*refs):
        combine_kernel(rank, *refs)

    rows = own.shape[0] + 2 * rank
    return pl.pallas_call(
        kernel,
        out_shape=jax.ShapeDtypeStruct((copies, rows, LANES), BF16),
        compiler_params=params(),
    )(own, other)


def finish_kernel(rank, blocks, parts_ref, *refs):
    slice_refs = refs[:blocks]
    down_ref, up_ref = refs[blocks:]
    size = rank * blocks
    tiles = size // LANES
    near = parts_ref.shape[0]
    position = lax.axis_index("section")
    own_half = lax.axis_index("dp") // near
    total = parts_ref[0, 4 * rank :].astype(F32)
    for member in range(1, near):
        total += parts_ref[member, 4 * rank :].astype(F32)

    def unfold(first):
        return jnp.concatenate(
            [total[(first + tile) * rank : (first + tile + 1) * rank] for tile in range(tiles)], axis=1
        )

    both_up, crossed = unfold(0), unfold(tiles)
    place = (lax.broadcasted_iota(jnp.int32, (rank, size), 1) // rank) ^ position
    below = jnp.where(place < position, crossed, 0.0)
    above = jnp.where(place > position, crossed, 0.0)
    wide = [ref[...].astype(F32) for ref in slice_refs]

    def stacked(first, count):
        return jnp.concatenate([piece[first : first + count] for piece in wide], axis=0).astype(BF16)

    result = jnp.zeros((2 * rank, slice_refs[0].shape[1]), F32)
    for half in range(2):
        start = pl.multiple_of((own_half ^ half) * 2 * rank, 16)
        for member in range(0, near, 2):
            pair = [parts_ref[member + i, pl.ds(start, 2 * rank)] for i in range(2)]
            bands = [stacked(8 * (half * near + member + i), 8) for i in range(2)]
            result += dot_nn(jnp.concatenate(pair, axis=1), jnp.concatenate(bands, axis=0))
    rows = 16 * near
    all_down = stacked(rows, rank)
    all_up = stacked(rows + rank, rank)
    high, low = split(jnp.concatenate([below, both_up], axis=0))
    sums = dot_nn(jnp.concatenate([high, low], axis=0), all_up)
    result += sums[0 : 2 * rank] + sums[2 * rank :]
    high, low = split(jnp.concatenate([above, jnp.zeros((8, size), F32)], axis=0))
    sums = dot_nn(jnp.concatenate([high, low], axis=0), all_down)
    cross = sums[0:rank] + sums[rank + 8 : 2 * rank + 8]
    down_ref[0] = result[0:rank]
    up_ref[0] = result[rank : 2 * rank] + cross


def finish(parts, slices, rank):
    blocks = len(slices)
    width = slices[0].shape[1]

    def kernel(*refs):
        finish_kernel(rank, blocks, *refs)

    shape = jax.ShapeDtypeStruct((1, rank, width), F32)
    return pl.pallas_call(
        kernel, out_shape=[shape, shape], compiler_params=params()
    )(parts, *slices)


def moved(value, axis, distance, count):
    return lax.ppermute(value, axis, [(i, i ^ distance) for i in range(count)])


def swapped(value, distance, count):
    return moved(value, "section", distance, count)


def shards(inputs, down_proj, up_proj):
    sections = lax.axis_size("section")
    members = lax.axis_size("dp")
    position = lax.axis_index("section")
    member = lax.axis_index("dp")
    own_down, own_up = down_proj[0], up_proj[0]
    rank, features = own_down.shape
    width = features // members
    pipes, micro, count = inputs.shape[:3]
    normalizer = float(micro * count * members)
    all_rows = inputs.reshape(pipes * micro * count, features)

    route = [
        (partner(s, d, sections) * members + d, s * members + d)
        for s in range(sections)
        for d in range(members)
    ]
    receiver = partner_of(position, member, sections)
    outgoing = jnp.where(receiver >= position, own_up, own_down)
    other = lax.ppermute(outgoing, ("section", "dp"), route)

    share = lax.dynamic_index_in_dim(
        inputs.reshape(sections, count, features), position, 0, keepdims=False
    )
    weight = jnp.concatenate(
        [lax.dynamic_slice_in_dim(w, member * width, width, 1) for w in (own_down, own_up)], axis=0
    )
    both, square = project(all_rows, own_down, own_up)
    other, share, weight, both, square = lax.optimization_barrier(
        (other, share, weight, both, square)
    )

    products = lax.all_to_all(pair_products(own_up, other, share, members), "dp", 0, 0)
    grid, share = order_blocks(products, both, weight, rank, sections)
    grid = lax.all_to_all(grid, "section", 0, 0)

    half = sections // 2
    last = half - 2
    early = (0, 2, last)
    slices = {d: swapped(share, d, sections) for d in (2, last, half)}
    later = {d: swapped(share, d, sections) for d in range(4, last, 2)}
    parts = run_chain(grid, square, rank, features, normalizer)
    parts, slices = lax.optimization_barrier((parts, slices))

    line = members // 2
    other = moved(parts, "dp", line, members)
    parts, other, slices, later = lax.optimization_barrier((parts, other, slices, later))
    slices = {0: share, **slices, **later}
    for d in (2, last):
        slices[half + d] = swapped(slices[half], d, sections)
    for d in range(4, last, 2):
        slices[half + d] = swapped(slices[d], half, sections)
    for d in early:
        slices[d + 1] = swapped(slices[d], 1, sections)
    parts = combine(parts, other, rank, line)
    groups = [list(range(start, start + line)) for start in (0, line)]
    parts = lax.all_to_all(parts, "dp", 0, 0, axis_index_groups=groups)
    parts, slices = lax.optimization_barrier((parts, slices))
    for d in range(0, sections, 2):
        if d not in early:
            slices[d + 1] = swapped(slices[d], 1, sections)
    return finish(parts, [slices[d] for d in range(sections)], rank)


def solution(mesh):
    placed = (P(None, None, "dp", None), P("section", None, None), P("section", None, None))
    return jax.shard_map(
        shards,
        mesh=mesh,
        in_specs=placed,
        out_specs=(P("section", None, "dp"), P("section", None, "dp")),
        check_vma=False,
    )
```

```python
import jax
import jax.numpy as jnp
from jax import lax
from jax.experimental import pallas as pl
from jax.experimental.pallas import tpu as pltpu
from jax.sharding import PartitionSpec as P

EPS = 1e-05
LANES = 128
F32 = jnp.float32
BF16 = jnp.bfloat16


def split(value):
    high = value.astype(BF16)
    return high, (value - high.astype(F32)).astype(BF16)


def dot_nn(left, right):
    return lax.dot_general(left, right, (((1,), (0,)), ((), ())), preferred_element_type=F32)


def dot_nt(left, right):
    return lax.dot_general(left, right, (((1,), (1,)), ((), ())), preferred_element_type=F32)


def params(megabytes=12):
    return pltpu.CompilerParams(vmem_limit_bytes=megabytes * 1024 * 1024)


def project_kernel(x_ref, down_ref, up_ref, both_ref, square_ref):
    rank, features = down_ref.shape
    width = 1536
    down = jnp.zeros((rank, LANES), F32)
    up = jnp.zeros((rank, LANES), F32)
    total = jnp.zeros((LANES, LANES), F32)
    for start in range(0, features, width):
        rows = x_ref[:, start : start + width]
        down += dot_nt(down_ref[:, start : start + width], rows)
        up += dot_nt(up_ref[:, start : start + width], rows)
        wide = rows.astype(F32)
        for tile in range(0, wide.shape[1], LANES):
            part = wide[:, tile : tile + LANES]
            total += part * part
    both_ref[0:rank] = down
    both_ref[rank : 2 * rank] = up
    square_ref[...] = jnp.sum(total.T, axis=0, keepdims=True)


def project(rows, down, up):
    rank = down.shape[0]
    return pl.pallas_call(
        project_kernel,
        out_shape=[
            jax.ShapeDtypeStruct((2 * rank, LANES), F32),
            jax.ShapeDtypeStruct((1, LANES), F32),
        ],
        compiler_params=params(),
    )(rows, down, up)


def pair_kernel(own_ref, other_ref, share_ref, out_ref, pad_ref):
    rank, features = own_ref.shape
    members = out_ref.shape[0]
    pad_ref[...] = jnp.zeros_like(pad_ref)
    pad_ref[:, 0:rank] = dot_nt(own_ref[...], other_ref[...])
    packed = pad_ref[0:8]
    for group in range(1, rank // 8):
        packed += pltpu.roll(pad_ref[8 * group : 8 * group + 8], rank * group, 1)
    head = jnp.concatenate([packed, jnp.zeros_like(packed)], axis=0)
    tiles = features // members // LANES
    for member in range(members):
        parts = [head]
        for tile in range(member * tiles, (member + 1) * tiles):
            parts.append(share_ref[:, tile * LANES : (tile + 1) * LANES].astype(F32))
        out_ref[member] = jnp.concatenate(parts, axis=0).astype(BF16)


def pair_products(own, other, share, members):
    rank, features = own.shape
    rows = 16 + 8 * (features // members // LANES)
    return pl.pallas_call(
        pair_kernel,
        out_shape=jax.ShapeDtypeStruct((members, rows, LANES), BF16),
        scratch_shapes=[pltpu.VMEM((rank, LANES), F32)],
        compiler_params=params(),
    )(own, other, share)


def partner(position, member, sections):
    return position ^ member ^ ((sections // 2 + sections // 4) * (position & 1))


def partner_of(position, member, sections):
    mixed = position ^ member
    return mixed ^ ((sections // 2 + sections // 4) * (mixed & 1))


def order_kernel(rank, blocks, in_ref, both_ref, weight_ref, out_ref, share_ref, work_ref):
    position = lax.axis_index("section")
    lane = lax.broadcasted_iota(jnp.int32, (8, LANES), 1)
    tiles = rank * blocks // LANES
    pieces = [in_ref[partner(position, t, blocks)].astype(F32)[0:8] for t in range(blocks)]
    bands = []
    for member in range(in_ref.shape[0]):
        piece = in_ref[member].astype(F32)
        band = [piece[row : row + 8] for row in range(16, piece.shape[0], 8)]
        bands.append(jnp.concatenate(band, axis=1))
    rows = 8 * in_ref.shape[0]
    share_ref[0:rows] = jnp.concatenate(bands, axis=0).astype(BF16)
    share_ref[rows:] = weight_ref[...]
    for group in range(rank // 8):
        turned = [pltpu.roll(pieces[t], (rank * (t - group)) % LANES, 1) for t in range(blocks)]
        for tile in range(tiles):
            place = (lane + tile * LANES) // rank
            value = jnp.zeros((8, LANES), F32)
            for t in range(blocks):
                if rank * t < (tile + 1) * LANES and rank * (t + 1) > tile * LANES:
                    value = jnp.where(place == t, turned[t], value)
            work_ref[tile * rank + 8 * group : tile * rank + 8 * group + 8] = value
    work_ref[tiles * rank : (tiles + 2) * rank] = both_ref[...]
    filled = (tiles + 2) * rank
    if filled < work_ref.shape[0]:
        work_ref[filled:] = jnp.zeros((work_ref.shape[0] - filled, LANES), F32)
    payload = work_ref[...].astype(BF16)
    for copy in range(out_ref.shape[0]):
        out_ref[copy] = payload


def order_blocks(gathered, both, weight, rank, copies):
    blocks = gathered.shape[0]

    def kernel(*refs):
        order_kernel(rank, blocks, *refs)

    rows = -(-(rank * blocks // LANES + 2) * rank // 16) * 16
    members, height = gathered.shape[:2]
    return pl.pallas_call(
        kernel,
        out_shape=[
            jax.ShapeDtypeStruct((copies, rows, LANES), BF16),
            jax.ShapeDtypeStruct((8 * members + 2 * rank, (height - 16) // 8 * LANES), BF16),
        ],
        scratch_shapes=[pltpu.VMEM((rows, LANES), F32)],
        compiler_params=params(),
    )(gathered, both, weight)


def chain_kernel(rank, blocks, features, normalizer, grid_ref, square_ref, out_ref, *rest):
    plain_ref, turned_ref, act_ref, scaled_ref, grad_ref, skip_ref = rest
    size = rank * blocks
    tiles = size // LANES
    received = [grid_ref[b].astype(F32) for b in range(blocks)]
    whole = jnp.concatenate(
        [
            jnp.concatenate(
                [piece[tile * rank : (tile + 1) * rank] for tile in range(tiles)], axis=1
            )
            for piece in received
        ],
        axis=0,
    )
    plain_ref[...] = whole.astype(BF16)
    turned_ref[...] = whole.T.astype(BF16)

    def span(b):
        first = rank * b // LANES
        last = (rank * b + rank - 1) // LANES
        return first, last

    def columns(ref, b, start, stop):
        first, last = span(b)
        return ref[start:stop, first * LANES : (last + 1) * LANES]

    def placed(b, value):
        first, last = span(b)
        before = rank * b - first * LANES
        after = (last + 1) * LANES - rank * (b + 1)
        parts = []
        if before:
            parts.append(jnp.zeros((before, LANES), F32))
        parts.append(value)
        if after:
            parts.append(jnp.zeros((after, LANES), F32))
        return jnp.concatenate(parts, axis=0).astype(BF16)

    narrow, hidden = [], []
    for piece in received:
        narrow.append(piece[tiles * rank : (tiles + 1) * rank])
        hidden.append(piece[(tiles + 1) * rank : (tiles + 2) * rank])
    initial = list(hidden)
    square = square_ref[...]
    inverses, acts, pres, slopes, ends = [], [], [], [], []
    for b in range(blocks):
        inverse = lax.rsqrt(square / features + EPS)
        pre = narrow[b] * inverse
        sigmoid = 1.0 / (1.0 + jnp.exp(-pre))
        act = (pre * sigmoid).astype(BF16).astype(F32)
        act_ref[rank * b : rank * (b + 1)] = act
        inverses.append(inverse)
        acts.append(act)
        pres.append(pre)
        slopes.append(sigmoid * (1.0 + pre * (1.0 - sigmoid)))
        right = placed(b, act)
        if b + 1 < blocks:
            start = rank * (b + 1) // 16 * 16
            update = dot_nn(columns(turned_ref, b, start, size), right)
            for k in range(b + 1, blocks):
                narrow[k] = narrow[k] + update[rank * k - start : rank * (k + 1) - start]
        start = rank * b // 16 * 16
        update = dot_nn(columns(plain_ref, b, start, size), right)
        own = update[rank * b - start : rank * (b + 1) - start]
        for k in range(b + 1, blocks):
            hidden[k] = hidden[k] + update[rank * k - start : rank * (k + 1) - start]
        square = square + jnp.sum(act * (2.0 * hidden[b] + own), axis=0, keepdims=True)
        ends.append(hidden[b] + own)

    back = [jnp.zeros((rank, LANES), F32) for _ in range(blocks)]
    decay = jnp.zeros((1, LANES), F32)
    for k in reversed(range(blocks)):
        weight = 1.0 / normalizer - decay
        scaled = acts[k] * weight
        scaled_ref[rank * k : rank * (k + 1)] = scaled
        skip_ref[rank * k : rank * (k + 1)] = -decay * acts[k]
        incoming = ends[k] * weight - initial[k] / normalizer + back[k]
        grad = (incoming * slopes[k] * inverses[k]).astype(BF16).astype(F32)
        grad_ref[rank * k : rank * (k + 1)] = grad
        decay = decay + inverses[k] / features * jnp.sum(grad * pres[k], axis=0, keepdims=True)
        if k:
            stop = -(-rank * k // 16) * 16
            coarse = scaled.astype(BF16).astype(F32)
            fine = scaled - coarse
            update = (
                dot_nn(columns(turned_ref, k, 0, stop), placed(k, coarse))
                + dot_nn(columns(turned_ref, k, 0, stop), placed(k, fine))
                + dot_nn(columns(plain_ref, k, 0, stop), placed(k, grad))
            )
            for b in range(k):
                back[b] = back[b] + update[rank * b : rank * (b + 1)]

    position = lax.axis_index("section")
    mine = pl.ds(pl.multiple_of(position * rank, 8), rank)
    own_act = act_ref[mine].astype(BF16)
    own_high, own_low = split(scaled_ref[mine])
    own_grad = grad_ref[mine].astype(BF16)
    all_act = act_ref[...].astype(BF16)
    all_high, all_low = split(scaled_ref[...])
    all_grad = grad_ref[...].astype(BF16)
    place = lax.broadcasted_iota(jnp.int32, (rank, size), 1) // rank
    later = dot_nt(own_act, all_high) + dot_nt(own_act, all_low)
    earlier = dot_nt(own_high, all_act) + dot_nt(own_low, all_act)
    both_up = jnp.where(place >= position, later, earlier)
    crossed = jnp.where(
        place < position,
        dot_nt(own_grad, all_act),
        jnp.where(place > position, dot_nt(own_act, all_grad), 0.0),
    )
    groups = LANES // 8
    source = lax.broadcasted_iota(jnp.int32, (LANES, LANES), 0)
    target = lax.broadcasted_iota(jnp.int32, (LANES, LANES), 1)
    moved = source == target ^ (position * (LANES // groups))
    rows = jnp.concatenate([grad_ref[mine], skip_ref[mine]], axis=0).astype(BF16)
    rows = dot_nn(rows, jnp.where(moved, 1.0, 0.0).astype(BF16))
    source = lax.broadcasted_iota(jnp.int32, (size, size), 0)
    target = lax.broadcasted_iota(jnp.int32, (size, size), 1)
    block = target // rank
    moved = source == target + rank * ((block ^ position) - block)
    sums = jnp.concatenate([both_up, crossed], axis=0).astype(BF16)
    sums = dot_nn(sums, jnp.where(moved, 1.0, 0.0).astype(BF16))
    pieces = [rows]
    for value in (sums[0:rank], sums[rank : 2 * rank]):
        pieces += [value[:, tile * LANES : (tile + 1) * LANES] for tile in range(tiles)]
    out_ref[...] = jnp.concatenate(pieces, axis=0).astype(BF16)


def run_chain(grid, square, rank, features, normalizer):
    blocks = grid.shape[0]
    size = rank * blocks
    rows = 2 * rank + 2 * (size // LANES) * rank

    def kernel(*refs):
        chain_kernel(rank, blocks, features, normalizer, *refs)

    narrow = pltpu.VMEM((size, LANES), F32)
    square_matrix = pltpu.VMEM((size, size), BF16)
    return pl.pallas_call(
        kernel,
        out_shape=jax.ShapeDtypeStruct((rows, LANES), BF16),
        scratch_shapes=[square_matrix, square_matrix, narrow, narrow, narrow, narrow],
        compiler_params=params(),
    )(grid, square)


def combine_kernel(rank, own_ref, other_ref, out_ref):
    own, other = own_ref[...], other_ref[...]
    both = own.astype(F32) + other.astype(F32)
    payload = jnp.concatenate(
        [own[0 : 2 * rank], other[0 : 2 * rank], both[2 * rank :].astype(BF16)], axis=0
    )
    for copy in range(out_ref.shape[0]):
        out_ref[copy] = payload


def combine(own, other, rank, copies):
    def kernel(*refs):
        combine_kernel(rank, *refs)

    rows = own.shape[0] + 2 * rank
    return pl.pallas_call(
        kernel,
        out_shape=jax.ShapeDtypeStruct((copies, rows, LANES), BF16),
        compiler_params=params(),
    )(own, other)


def finish_kernel(rank, blocks, parts_ref, *refs):
    slice_refs = refs[:blocks]
    down_ref, up_ref = refs[blocks:]
    size = rank * blocks
    tiles = size // LANES
    near = parts_ref.shape[0]
    position = lax.axis_index("section")
    own_half = lax.axis_index("dp") // near
    total = parts_ref[0, 4 * rank :].astype(F32)
    for member in range(1, near):
        total += parts_ref[member, 4 * rank :].astype(F32)

    def unfold(first):
        return jnp.concatenate(
            [total[(first + tile) * rank : (first + tile + 1) * rank] for tile in range(tiles)], axis=1
        )

    both_up, crossed = unfold(0), unfold(tiles)
    place = (lax.broadcasted_iota(jnp.int32, (rank, size), 1) // rank) ^ position
    below = jnp.where(place < position, crossed, 0.0)
    above = jnp.where(place > position, crossed, 0.0)
    wide = [ref[...].astype(F32) for ref in slice_refs]

    def stacked(first, count):
        return jnp.concatenate([piece[first : first + count] for piece in wide], axis=0).astype(BF16)

    result = jnp.zeros((2 * rank, slice_refs[0].shape[1]), F32)
    for half in range(2):
        start = pl.multiple_of((own_half ^ half) * 2 * rank, 16)
        for member in range(0, near, 2):
            pair = [parts_ref[member + i, pl.ds(start, 2 * rank)] for i in range(2)]
            bands = [stacked(8 * (half * near + member + i), 8) for i in range(2)]
            result += dot_nn(jnp.concatenate(pair, axis=1), jnp.concatenate(bands, axis=0))
    rows = 16 * near
    all_down = stacked(rows, rank)
    all_up = stacked(rows + rank, rank)
    high, low = split(jnp.concatenate([below, both_up], axis=0))
    sums = dot_nn(jnp.concatenate([high, low], axis=0), all_up)
    result += sums[0 : 2 * rank] + sums[2 * rank :]
    high, low = split(jnp.concatenate([above, jnp.zeros((8, size), F32)], axis=0))
    sums = dot_nn(jnp.concatenate([high, low], axis=0), all_down)
    cross = sums[0:rank] + sums[rank + 8 : 2 * rank + 8]
    down_ref[0] = result[0:rank]
    up_ref[0] = result[rank : 2 * rank] + cross


def finish(parts, slices, rank):
    blocks = len(slices)
    width = slices[0].shape[1]

    def kernel(*refs):
        finish_kernel(rank, blocks, *refs)

    shape = jax.ShapeDtypeStruct((1, rank, width), F32)
    return pl.pallas_call(
        kernel, out_shape=[shape, shape], compiler_params=params()
    )(parts, *slices)


def moved(value, axis, distance, count):
    return lax.ppermute(value, axis, [(i, i ^ distance) for i in range(count)])


def swapped(value, distance, count):
    return moved(value, "section", distance, count)


def shards(inputs, down_proj, up_proj):
    sections = lax.axis_size("section")
    members = lax.axis_size("dp")
    position = lax.axis_index("section")
    member = lax.axis_index("dp")
    own_down, own_up = down_proj[0], up_proj[0]
    rank, features = own_down.shape
    width = features // members
    pipes, micro, count = inputs.shape[:3]
    normalizer = float(micro * count * members)
    all_rows = inputs.reshape(pipes * micro * count, features)

    route = [
        (partner(s, d, sections) * members + d, s * members + d)
        for s in range(sections)
        for d in range(members)
    ]
    receiver = partner_of(position, member, sections)
    outgoing = jnp.where(receiver >= position, own_up, own_down)
    other = lax.ppermute(outgoing, ("section", "dp"), route)

    share = lax.dynamic_index_in_dim(
        inputs.reshape(sections, count, features), position, 0, keepdims=False
    )
    weight = jnp.concatenate(
        [lax.dynamic_slice_in_dim(w, member * width, width, 1) for w in (own_down, own_up)], axis=0
    )
    both, square = project(all_rows, own_down, own_up)
    other, share, weight, both, square = lax.optimization_barrier(
        (other, share, weight, both, square)
    )

    products = lax.all_to_all(pair_products(own_up, other, share, members), "dp", 0, 0)
    grid, share = order_blocks(products, both, weight, rank, sections)
    grid = lax.all_to_all(grid, "section", 0, 0)

    half = sections // 2
    last = half - 2
    early = (0, 2, 4, last)
    slices = {d: swapped(share, d, sections) for d in (2, last, half)}
    later = {d: swapped(share, d, sections) for d in range(4, last, 2)}
    parts = run_chain(grid, square, rank, features, normalizer)
    parts, slices = lax.optimization_barrier((parts, slices))

    line = members // 2
    other = moved(parts, "dp", line, members)
    parts, other, slices, later = lax.optimization_barrier((parts, other, slices, later))
    slices = {0: share, **slices, **later}
    for d in (2, last):
        slices[half + d] = swapped(slices[half], d, sections)
    for d in range(4, last, 2):
        slices[half + d] = swapped(slices[d], half, sections)
    for d in early:
        slices[d + 1] = swapped(slices[d], 1, sections)
    parts = combine(parts, other, rank, line)
    groups = [list(range(start, start + line)) for start in (0, line)]
    parts = lax.all_to_all(parts, "dp", 0, 0, axis_index_groups=groups)
    parts, slices = lax.optimization_barrier((parts, slices))
    for d in range(0, sections, 2):
        if d not in early:
            slices[d + 1] = swapped(slices[d], 1, sections)
    return finish(parts, [slices[d] for d in range(sections)], rank)


def solution(mesh):
    placed = (P(None, None, "dp", None), P("section", None, None), P("section", None, None))
    return jax.shard_map(
        shards,
        mesh=mesh,
        in_specs=placed,
        out_specs=(P("section", None, "dp"), P("section", None, "dp")),
        check_vma=False,
    )
```

```python
import jax
import jax.numpy as jnp
from jax import lax
from jax.experimental import pallas as pl
from jax.experimental.pallas import tpu as pltpu
from jax.sharding import PartitionSpec as P

EPS = 1e-05
LANES = 128
F32 = jnp.float32
BF16 = jnp.bfloat16


def split(value):
    high = value.astype(BF16)
    return high, (value - high.astype(F32)).astype(BF16)


def dot_nn(left, right):
    return lax.dot_general(left, right, (((1,), (0,)), ((), ())), preferred_element_type=F32)


def dot_nt(left, right):
    return lax.dot_general(left, right, (((1,), (1,)), ((), ())), preferred_element_type=F32)


def params(megabytes=12):
    return pltpu.CompilerParams(vmem_limit_bytes=megabytes * 1024 * 1024)


def project_kernel(x_ref, down_ref, up_ref, both_ref, square_ref):
    rank, features = down_ref.shape
    width = 1536
    down = jnp.zeros((rank, LANES), F32)
    up = jnp.zeros((rank, LANES), F32)
    total = jnp.zeros((LANES, LANES), F32)
    for start in range(0, features, width):
        rows = x_ref[:, start : start + width]
        down += dot_nt(down_ref[:, start : start + width], rows)
        up += dot_nt(up_ref[:, start : start + width], rows)
        wide = rows.astype(F32)
        for tile in range(0, wide.shape[1], LANES):
            part = wide[:, tile : tile + LANES]
            total += part * part
    both_ref[0:rank] = down
    both_ref[rank : 2 * rank] = up
    square_ref[...] = jnp.sum(total.T, axis=0, keepdims=True)


def project(rows, down, up):
    rank = down.shape[0]
    return pl.pallas_call(
        project_kernel,
        out_shape=[
            jax.ShapeDtypeStruct((2 * rank, LANES), F32),
            jax.ShapeDtypeStruct((1, LANES), F32),
        ],
        compiler_params=params(),
    )(rows, down, up)


def pair_kernel(own_ref, other_ref, share_ref, out_ref, pad_ref):
    rank, features = own_ref.shape
    members = out_ref.shape[0]
    pad_ref[...] = jnp.zeros_like(pad_ref)
    pad_ref[:, 0:rank] = dot_nt(own_ref[...], other_ref[...])
    packed = pad_ref[0:8]
    for group in range(1, rank // 8):
        packed += pltpu.roll(pad_ref[8 * group : 8 * group + 8], rank * group, 1)
    head = jnp.concatenate([packed, jnp.zeros_like(packed)], axis=0)
    tiles = features // members // LANES
    for member in range(members):
        parts = [head]
        for tile in range(member * tiles, (member + 1) * tiles):
            parts.append(share_ref[:, tile * LANES : (tile + 1) * LANES].astype(F32))
        out_ref[member] = jnp.concatenate(parts, axis=0).astype(BF16)


def pair_products(own, other, share, members):
    rank, features = own.shape
    rows = 16 + 8 * (features // members // LANES)
    return pl.pallas_call(
        pair_kernel,
        out_shape=jax.ShapeDtypeStruct((members, rows, LANES), BF16),
        scratch_shapes=[pltpu.VMEM((rank, LANES), F32)],
        compiler_params=params(),
    )(own, other, share)


def partner(position, member, sections):
    return position ^ member ^ ((sections // 2 + sections // 4) * (position & 1))


def partner_of(position, member, sections):
    mixed = position ^ member
    return mixed ^ ((sections // 2 + sections // 4) * (mixed & 1))


def order_kernel(rank, blocks, in_ref, both_ref, weight_ref, out_ref, share_ref, work_ref):
    position = lax.axis_index("section")
    lane = lax.broadcasted_iota(jnp.int32, (8, LANES), 1)
    tiles = rank * blocks // LANES
    pieces = [in_ref[partner(position, t, blocks)].astype(F32)[0:8] for t in range(blocks)]
    bands = []
    for member in range(in_ref.shape[0]):
        piece = in_ref[member].astype(F32)
        band = [piece[row : row + 8] for row in range(16, piece.shape[0], 8)]
        bands.append(jnp.concatenate(band, axis=1))
    rows = 8 * in_ref.shape[0]
    share_ref[0:rows] = jnp.concatenate(bands, axis=0).astype(BF16)
    share_ref[rows:] = weight_ref[...]
    for group in range(rank // 8):
        turned = [pltpu.roll(pieces[t], (rank * (t - group)) % LANES, 1) for t in range(blocks)]
        for tile in range(tiles):
            place = (lane + tile * LANES) // rank
            value = jnp.zeros((8, LANES), F32)
            for t in range(blocks):
                if rank * t < (tile + 1) * LANES and rank * (t + 1) > tile * LANES:
                    value = jnp.where(place == t, turned[t], value)
            work_ref[tile * rank + 8 * group : tile * rank + 8 * group + 8] = value
    work_ref[tiles * rank : (tiles + 2) * rank] = both_ref[...]
    filled = (tiles + 2) * rank
    if filled < work_ref.shape[0]:
        work_ref[filled:] = jnp.zeros((work_ref.shape[0] - filled, LANES), F32)
    payload = work_ref[...].astype(BF16)
    for copy in range(out_ref.shape[0]):
        out_ref[copy] = payload


def order_blocks(gathered, both, weight, rank, copies):
    blocks = gathered.shape[0]

    def kernel(*refs):
        order_kernel(rank, blocks, *refs)

    rows = -(-(rank * blocks // LANES + 2) * rank // 16) * 16
    members, height = gathered.shape[:2]
    return pl.pallas_call(
        kernel,
        out_shape=[
            jax.ShapeDtypeStruct((copies, rows, LANES), BF16),
            jax.ShapeDtypeStruct((8 * members + 2 * rank, (height - 16) // 8 * LANES), BF16),
        ],
        scratch_shapes=[pltpu.VMEM((rows, LANES), F32)],
        compiler_params=params(),
    )(gathered, both, weight)


def chain_kernel(rank, blocks, features, normalizer, grid_ref, square_ref, out_ref, *rest):
    plain_ref, turned_ref, act_ref, scaled_ref, grad_ref, skip_ref = rest
    size = rank * blocks
    tiles = size // LANES
    received = [grid_ref[b].astype(F32) for b in range(blocks)]
    whole = jnp.concatenate(
        [
            jnp.concatenate(
                [piece[tile * rank : (tile + 1) * rank] for tile in range(tiles)], axis=1
            )
            for piece in received
        ],
        axis=0,
    )
    plain_ref[...] = whole.astype(BF16)
    turned_ref[...] = whole.T.astype(BF16)

    def span(b):
        first = rank * b // LANES
        last = (rank * b + rank - 1) // LANES
        return first, last

    def columns(ref, b, start, stop):
        first, last = span(b)
        return ref[start:stop, first * LANES : (last + 1) * LANES]

    def placed(b, value):
        first, last = span(b)
        before = rank * b - first * LANES
        after = (last + 1) * LANES - rank * (b + 1)
        parts = []
        if before:
            parts.append(jnp.zeros((before, LANES), F32))
        parts.append(value)
        if after:
            parts.append(jnp.zeros((after, LANES), F32))
        return jnp.concatenate(parts, axis=0).astype(BF16)

    narrow, hidden = [], []
    for piece in received:
        narrow.append(piece[tiles * rank : (tiles + 1) * rank])
        hidden.append(piece[(tiles + 1) * rank : (tiles + 2) * rank])
    initial = list(hidden)
    square = square_ref[...]
    inverses, acts, pres, slopes, ends = [], [], [], [], []
    for b in range(blocks):
        inverse = lax.rsqrt(square / features + EPS)
        pre = narrow[b] * inverse
        sigmoid = 1.0 / (1.0 + jnp.exp(-pre))
        act = (pre * sigmoid).astype(BF16).astype(F32)
        act_ref[rank * b : rank * (b + 1)] = act
        inverses.append(inverse)
        acts.append(act)
        pres.append(pre)
        slopes.append(sigmoid * (1.0 + pre * (1.0 - sigmoid)))
        right = placed(b, act)
        if b + 1 < blocks:
            start = rank * (b + 1) // 16 * 16
            update = dot_nn(columns(turned_ref, b, start, size), right)
            for k in range(b + 1, blocks):
                narrow[k] = narrow[k] + update[rank * k - start : rank * (k + 1) - start]
        start = rank * b // 16 * 16
        update = dot_nn(columns(plain_ref, b, start, size), right)
        own = update[rank * b - start : rank * (b + 1) - start]
        for k in range(b + 1, blocks):
            hidden[k] = hidden[k] + update[rank * k - start : rank * (k + 1) - start]
        square = square + jnp.sum(act * (2.0 * hidden[b] + own), axis=0, keepdims=True)
        ends.append(hidden[b] + own)

    back = [jnp.zeros((rank, LANES), F32) for _ in range(blocks)]
    decay = jnp.zeros((1, LANES), F32)
    for k in reversed(range(blocks)):
        weight = 1.0 / normalizer - decay
        scaled = acts[k] * weight
        scaled_ref[rank * k : rank * (k + 1)] = scaled
        skip_ref[rank * k : rank * (k + 1)] = -decay * acts[k]
        incoming = ends[k] * weight - initial[k] / normalizer + back[k]
        grad = (incoming * slopes[k] * inverses[k]).astype(BF16).astype(F32)
        grad_ref[rank * k : rank * (k + 1)] = grad
        decay = decay + inverses[k] / features * jnp.sum(grad * pres[k], axis=0, keepdims=True)
        if k:
            stop = -(-rank * k // 16) * 16
            coarse = scaled.astype(BF16).astype(F32)
            fine = scaled - coarse
            update = (
                dot_nn(columns(turned_ref, k, 0, stop), placed(k, coarse))
                + dot_nn(columns(turned_ref, k, 0, stop), placed(k, fine))
                + dot_nn(columns(plain_ref, k, 0, stop), placed(k, grad))
            )
            for b in range(k):
                back[b] = back[b] + update[rank * b : rank * (b + 1)]

    position = lax.axis_index("section")
    mine = pl.ds(pl.multiple_of(position * rank, 8), rank)
    own_act = act_ref[mine].astype(BF16)
    own_high, own_low = split(scaled_ref[mine])
    own_grad = grad_ref[mine].astype(BF16)
    all_act = act_ref[...].astype(BF16)
    all_high, all_low = split(scaled_ref[...])
    all_grad = grad_ref[...].astype(BF16)
    place = lax.broadcasted_iota(jnp.int32, (rank, size), 1) // rank
    later = dot_nt(own_act, all_high) + dot_nt(own_act, all_low)
    earlier = dot_nt(own_high, all_act) + dot_nt(own_low, all_act)
    both_up = jnp.where(place >= position, later, earlier)
    crossed = jnp.where(
        place < position,
        dot_nt(own_grad, all_act),
        jnp.where(place > position, dot_nt(own_act, all_grad), 0.0),
    )
    groups = LANES // 8
    source = lax.broadcasted_iota(jnp.int32, (LANES, LANES), 0)
    target = lax.broadcasted_iota(jnp.int32, (LANES, LANES), 1)
    moved = source == target ^ (position * (LANES // groups))
    rows = jnp.concatenate([grad_ref[mine], skip_ref[mine]], axis=0).astype(BF16)
    rows = dot_nn(rows, jnp.where(moved, 1.0, 0.0).astype(BF16))
    source = lax.broadcasted_iota(jnp.int32, (size, size), 0)
    target = lax.broadcasted_iota(jnp.int32, (size, size), 1)
    block = target // rank
    moved = source == target + rank * ((block ^ position) - block)
    sums = jnp.concatenate([both_up, crossed], axis=0).astype(BF16)
    sums = dot_nn(sums, jnp.where(moved, 1.0, 0.0).astype(BF16))
    pieces = [rows]
    for value in (sums[0:rank], sums[rank : 2 * rank]):
        pieces += [value[:, tile * LANES : (tile + 1) * LANES] for tile in range(tiles)]
    out_ref[...] = jnp.concatenate(pieces, axis=0).astype(BF16)


def run_chain(grid, square, rank, features, normalizer):
    blocks = grid.shape[0]
    size = rank * blocks
    rows = 2 * rank + 2 * (size // LANES) * rank

    def kernel(*refs):
        chain_kernel(rank, blocks, features, normalizer, *refs)

    narrow = pltpu.VMEM((size, LANES), F32)
    square_matrix = pltpu.VMEM((size, size), BF16)
    return pl.pallas_call(
        kernel,
        out_shape=jax.ShapeDtypeStruct((rows, LANES), BF16),
        scratch_shapes=[square_matrix, square_matrix, narrow, narrow, narrow, narrow],
        compiler_params=params(),
    )(grid, square)


def combine_kernel(rank, own_ref, other_ref, out_ref):
    own, other = own_ref[...], other_ref[...]
    both = own.astype(F32) + other.astype(F32)
    payload = jnp.concatenate(
        [own[0 : 2 * rank], other[0 : 2 * rank], both[2 * rank :].astype(BF16)], axis=0
    )
    for copy in range(out_ref.shape[0]):
        out_ref[copy] = payload


def combine(own, other, rank, copies):
    def kernel(*refs):
        combine_kernel(rank, *refs)

    rows = own.shape[0] + 2 * rank
    return pl.pallas_call(
        kernel,
        out_shape=jax.ShapeDtypeStruct((copies, rows, LANES), BF16),
        compiler_params=params(),
    )(own, other)


def finish_kernel(rank, blocks, parts_ref, *refs):
    slice_refs = refs[:blocks]
    down_ref, up_ref = refs[blocks:]
    size = rank * blocks
    tiles = size // LANES
    near = parts_ref.shape[0]
    position = lax.axis_index("section")
    own_half = lax.axis_index("dp") // near
    total = parts_ref[0, 4 * rank :].astype(F32)
    for member in range(1, near):
        total += parts_ref[member, 4 * rank :].astype(F32)

    def unfold(first):
        return jnp.concatenate(
            [total[(first + tile) * rank : (first + tile + 1) * rank] for tile in range(tiles)], axis=1
        )

    both_up, crossed = unfold(0), unfold(tiles)
    place = (lax.broadcasted_iota(jnp.int32, (rank, size), 1) // rank) ^ position
    below = jnp.where(place < position, crossed, 0.0)
    above = jnp.where(place > position, crossed, 0.0)
    wide = [ref[...].astype(F32) for ref in slice_refs]

    def stacked(first, count):
        return jnp.concatenate([piece[first : first + count] for piece in wide], axis=0).astype(BF16)

    result = jnp.zeros((2 * rank, slice_refs[0].shape[1]), F32)
    for half in range(2):
        start = pl.multiple_of((own_half ^ half) * 2 * rank, 16)
        for member in range(0, near, 2):
            pair = [parts_ref[member + i, pl.ds(start, 2 * rank)] for i in range(2)]
            bands = [stacked(8 * (half * near + member + i), 8) for i in range(2)]
            result += dot_nn(jnp.concatenate(pair, axis=1), jnp.concatenate(bands, axis=0))
    rows = 16 * near
    all_down = stacked(rows, rank)
    all_up = stacked(rows + rank, rank)
    high, low = split(jnp.concatenate([below, both_up], axis=0))
    sums = dot_nn(jnp.concatenate([high, low], axis=0), all_up)
    result += sums[0 : 2 * rank] + sums[2 * rank :]
    high, low = split(jnp.concatenate([above, jnp.zeros((8, size), F32)], axis=0))
    sums = dot_nn(jnp.concatenate([high, low], axis=0), all_down)
    cross = sums[0:rank] + sums[rank + 8 : 2 * rank + 8]
    down_ref[0] = result[0:rank]
    up_ref[0] = result[rank : 2 * rank] + cross


def finish(parts, slices, rank):
    blocks = len(slices)
    width = slices[0].shape[1]

    def kernel(*refs):
        finish_kernel(rank, blocks, *refs)

    shape = jax.ShapeDtypeStruct((1, rank, width), F32)
    return pl.pallas_call(
        kernel, out_shape=[shape, shape], compiler_params=params()
    )(parts, *slices)


def moved(value, axis, distance, count):
    return lax.ppermute(value, axis, [(i, i ^ distance) for i in range(count)])


def swapped(value, distance, count):
    return moved(value, "section", distance, count)


def shards(inputs, down_proj, up_proj):
    sections = lax.axis_size("section")
    members = lax.axis_size("dp")
    position = lax.axis_index("section")
    member = lax.axis_index("dp")
    own_down, own_up = down_proj[0], up_proj[0]
    rank, features = own_down.shape
    width = features // members
    pipes, micro, count = inputs.shape[:3]
    normalizer = float(micro * count * members)
    all_rows = inputs.reshape(pipes * micro * count, features)

    route = [
        (partner(s, d, sections) * members + d, s * members + d)
        for s in range(sections)
        for d in range(members)
    ]
    receiver = partner_of(position, member, sections)
    outgoing = jnp.where(receiver >= position, own_up, own_down)
    other = lax.ppermute(outgoing, ("section", "dp"), route)

    share = lax.dynamic_index_in_dim(
        inputs.reshape(sections, count, features), position, 0, keepdims=False
    )
    weight = jnp.concatenate(
        [lax.dynamic_slice_in_dim(w, member * width, width, 1) for w in (own_down, own_up)], axis=0
    )
    both, square = project(all_rows, own_down, own_up)
    other, share, weight, both, square = lax.optimization_barrier(
        (other, share, weight, both, square)
    )

    products = lax.all_to_all(pair_products(own_up, other, share, members), "dp", 0, 0)
    grid, share = order_blocks(products, both, weight, rank, sections)
    grid = lax.all_to_all(grid, "section", 0, 0)

    half = sections // 2
    last = half - 2
    early = (0, 2, last)
    slices = {d: swapped(share, d, sections) for d in (2, last, half)}
    later = {d: swapped(share, d, sections) for d in range(4, last, 2)}
    parts = run_chain(grid, square, rank, features, normalizer)
    parts, slices = lax.optimization_barrier((parts, slices))

    line = members // 2
    other = moved(parts, "dp", line, members)
    parts, other, slices, later = lax.optimization_barrier((parts, other, slices, later))
    slices = {0: share, **slices, **later}
    slices[half + last] = swapped(slices[half], last, sections)
    for d in range(2, last, 2):
        slices[half + d] = swapped(slices[d], half, sections)
    for d in early:
        slices[d + 1] = swapped(slices[d], 1, sections)
    parts = combine(parts, other, rank, line)
    groups = [list(range(start, start + line)) for start in (0, line)]
    parts = lax.all_to_all(parts, "dp", 0, 0, axis_index_groups=groups)
    parts, slices = lax.optimization_barrier((parts, slices))
    for d in range(0, sections, 2):
        if d not in early:
            slices[d + 1] = swapped(slices[d], 1, sections)
    return finish(parts, [slices[d] for d in range(sections)], rank)


def solution(mesh):
    placed = (P(None, None, "dp", None), P("section", None, None), P("section", None, None))
    return jax.shard_map(
        shards,
        mesh=mesh,
        in_specs=placed,
        out_specs=(P("section", None, "dp"), P("section", None, "dp")),
        check_vma=False,
    )
```
